32 devices in a mesh: lists: 4 (over z), seq: 8 (over y, x, core).
Axes of the slice: x: 2, y: 2, z: 4, core: 2. Of those that a mesh axis runs over, the one named last changes fastest.
Arguments:
- queries: bfloat16 [24576, 2048], P(('lists', 'seq')), parts along dimension 0, may hold values from -6 to 6
- key_rows: bfloat16 [24576, 2048], P(('lists', 'seq')), parts along dimension 0, may hold values from -6 to 6
- value_rows: bfloat16 [24576, 2048], P(('lists', 'seq')), parts along dimension 0, may hold values from -6 to 6
- out_grad: bfloat16 [24576, 2048], P(('lists', 'seq')), parts along dimension 0, may hold values from -6 to 6
Outputs:
- query_grad: bfloat16 [24576, 2048], P(('lists', 'seq')), parts along dimension 0
- key_grad: bfloat16 [24576, 2048], P(('lists', 'seq')), parts along dimension 0
- content_derivative: bfloat16 [24576, 2048], P(('lists', 'seq')), parts along dimension 0
The draws below stay inside these ranges and needn't reach their ends.
There are 4 independent parts, one for each index of `lists`. The reference program is written for one: setup_inputs(seed, part) draws one part's arguments, and reference() takes and returns one part's arrays. A program takes and returns all parts, laid end to end along the dimension named above; each array names one. Nothing has to cross between parts.
All inputs are finite; a program needn't handle non-finite values.
Results may differ from the reference program's by a relative error of at most 0.0049.
Values sent between devices are 32-bit elements; how exact they have to be, the bound alone decides.
No kernel may reach another device: no remote copies, remote signals or barrier semaphores. Data moves between devices by JAX's collectives and lax.ppermute only.
A program may use at most 192 MiB of HBM per device.

```python
import jax
import jax.numpy as jnp
from jax import lax

HEADS = 16
HEAD_DIM = 128
TOK_DEV = 768
WIDTH = 2048
LENGTH = 6144


def block_levels(stream_key, dims, cuts, least, high):
    def one(dim, shards_of):
        draws = jax.random.uniform(jax.random.fold_in(jax.random.fold_in(stream_key, 6), dim), (shards_of,), jnp.float32, least / len(cuts), high / len(cuts))
        return jnp.repeat(jnp.exp(draws), dims[dim] // shards_of).reshape((-1,) + (1,) * (len(dims) - dim - 1))

    factor_of = one(*cuts[0])
    for cut in cuts[1:]:
        factor_of = factor_of * one(*cut)
    return factor_of


def bell_draw(own_key, extent, spread, reach, split=(), kind=jnp.bfloat16):
    factor_of = block_levels(own_key, extent, split, -0.22, 0.18) if split else 1.0
    result = jax.random.normal(own_key, extent, jnp.float32) * spread * factor_of
    return jnp.minimum(jnp.maximum(result, -reach), reach).astype(kind)


def setup_inputs(seed: int = 0, part: int = 0) -> dict:
    key_of = jax.random.split(jax.random.key(seed), 5)
    part_splits = jax.random.split(jax.random.fold_in(key_of[4], part), 5)
    return {
        "queries": bell_draw(part_splits[0], (LENGTH, WIDTH), 1.0, 6.0, ((0, 8),)),
        "key_rows": bell_draw(part_splits[1], (LENGTH, WIDTH), 1.0, 6.0, ((0, 8),)),
        "value_rows": bell_draw(part_splits[2], (LENGTH, WIDTH), 1.0, 6.0, ((0, 8),)),
        "out_grad": bell_draw(part_splits[3], (LENGTH, WIDTH), 1.0, 6.0, ((0, 8),)),
    }


def reference(queries, key_rows, value_rows, out_grad):
    blocks = LENGTH // TOK_DEV
    scale_factor = (HEAD_DIM * LENGTH) ** -0.5
    dimensions_4 = (blocks, TOK_DEV, HEADS, HEAD_DIM)
    query_blocks = queries.reshape(dimensions_4)
    lookup_segments = key_rows.reshape(dimensions_4)
    value_blocks = value_rows.reshape(dimensions_4)
    grad_blocks = out_grad.reshape(dimensions_4)
    key_value_sum = jnp.einsum('bshk,bshv->bhkv', lookup_segments.astype(jnp.float32), value_blocks.astype(jnp.float32))
    query_output_sum = jnp.einsum('bthk,bthv->bhkv', query_blocks.astype(jnp.float32), grad_blocks.astype(jnp.float32))
    zero_state = jnp.zeros((1, HEADS, HEAD_DIM, HEAD_DIM), jnp.float32)
    cumulative_leading = jnp.concatenate([zero_state, jnp.cumsum(key_value_sum, axis=0)[:-1]], axis=0).astype(jnp.bfloat16)
    reverse_sum = jnp.cumsum(query_output_sum[::-1], axis=0)[::-1]
    suffix = jnp.concatenate([reverse_sum[1:], zero_state], axis=0).astype(jnp.bfloat16)
    later = jnp.arange(TOK_DEV, dtype=jnp.int32)
    causal = later[:, None] >= later[None, :]

    def one_block(items):
        query_one, key_one, value_one, grad_one, prefix_one, suffix_one = items
        query_float = query_one.astype(jnp.float32)
        key_float = key_one.astype(jnp.float32)
        value_float = value_one.astype(jnp.float32)
        gradient_float = grad_one.astype(jnp.float32)
        scores = jnp.einsum('thk,shk->hts', query_float, key_float)
        forward_weight_matrix = jnp.where(causal[None], scale_factor * scores, 0.0).astype(jnp.bfloat16).astype(jnp.float32)
        products = jnp.einsum('thv,shv->hts', gradient_float, value_float)
        weight_gradients = jnp.where(causal[None], scale_factor * products, 0.0).astype(jnp.bfloat16).astype(jnp.float32)
        prefix_float = prefix_one.astype(jnp.float32)
        suffix_float = suffix_one.astype(jnp.float32)
        query_portion = jnp.einsum('ynv,vyq->nyq', weight_gradients, key_float) + scale_factor * jnp.einsum('aro,rbo->arb', gradient_float, prefix_float)
        key_portion = jnp.einsum('eca,ceo->aeo', weight_gradients, query_float) + scale_factor * jnp.einsum('jan,aon->jao', value_float, suffix_float)
        value_portion = jnp.einsum('uno,nud->oud', forward_weight_matrix, gradient_float) + scale_factor * jnp.einsum('nam,amx->nax', key_float, suffix_float)
        return (query_portion.astype(jnp.bfloat16), key_portion.astype(jnp.bfloat16), value_portion.astype(jnp.bfloat16))

    query_grad, key_grad, content_derivative = lax.map(one_block, (query_blocks, lookup_segments, value_blocks, grad_blocks, cumulative_leading, suffix))
    flat = (LENGTH, HEADS * HEAD_DIM)
    return (query_grad.reshape(flat), key_grad.reshape(flat), content_derivative.reshape(flat))
```

```python
import functools

import jax
import jax.numpy as jnp
from jax import lax
from jax.experimental import pallas as pl
from jax.experimental.pallas import tpu as pltpu
from jax.sharding import PartitionSpec as P

HEADS = 16
HEAD_DIM = 128
HALF = HEADS // 2
COLUMNS = HALF * HEAD_DIM
CHUNKS = ((0, 4), (4, 8))
READS = 4
SUB = 256
PARTIAL = jnp.float32

TN = (((0,), (0,)), ((), ()))
NT = (((1,), (1,)), ((), ()))
NN = (((1,), (0,)), ((), ()))

IN_VMEM = pl.BlockSpec(memory_space=pltpu.VMEM)
ANYWHERE = pl.BlockSpec(memory_space=pl.ANY)
CHEAP = pl.CostEstimate(flops=1000, bytes_accessed=1000, transcendentals=0)
LONG = pl.CostEstimate(flops=2 * 10**10, bytes_accessed=1000, transcendentals=0)


def dot(left, right, dims):
    return lax.dot_general(left, right, dims, preferred_element_type=jnp.float32)


def state_of(heads):
    return pltpu.VMEM((2, heads, HEAD_DIM, HEAD_DIM), jnp.float32)


def my_core():
    return lax.rem(lax.axis_index("seq"), 2)


def comes_earlier(turn):
    pair = lax.div(lax.axis_index("seq"), 2)
    return jnp.bitwise_xor(pair, turn) < pair


def half_start(mine):
    half = my_core() if mine else 1 - my_core()
    return half * COLUMNS


def states_kernel(mine, *refs):
    sources, local, (sums, early, late, sems) = refs[:4], refs[-8:-4], refs[-4:]
    rows = local[0].shape[0]
    subs = rows // SUB
    width = READS * HEAD_DIM
    base = half_start(mine)
    copies = []
    for group in range(HALF // READS):
        for i in (1, 2, 0, 3):
            copy = pltpu.make_async_copy(
                sources[i].at[:, pl.ds(pl.multiple_of(base + group * width, width), width)],
                local[i].at[:, pl.ds(group * width, width)],
                sems.at[group, i],
            )
            copy.start()
            copies.append(copy)
    q, k, v, o = local
    for group in range(HALF // READS):
        for kind, (left, right) in enumerate(((k, v), (q, o))):
            copies[4 * group + 2 * kind].wait()
            copies[4 * group + 2 * kind + 1].wait()
            order = list(range(subs)) if kind == 0 else list(range(subs - 1, -1, -1))
            for head in range(group * READS, (group + 1) * READS):
                at = pl.ds(head * HEAD_DIM, HEAD_DIM)
                total = None
                for sub in order:
                    span = pl.ds(sub * SUB, SUB)
                    part = dot(left[span, at], right[span, at], TN)
                    total = part if total is None else total + part
                    if sub != order[-1]:
                        if kind == 0:
                            early[head, sub] = total
                        else:
                            late[head, sub - 1] = total
                sums[kind, head] = total


def states(mine, sources, after):
    rows = sources[0].shape[0]
    partial = pltpu.VMEM((HALF, rows // SUB - 1, HEAD_DIM, HEAD_DIM), jnp.float32)
    out = [pltpu.VMEM((rows, COLUMNS), jnp.bfloat16)] * 4 + [state_of(HALF), partial, partial]
    *local, sums, early, late = pl.pallas_call(
        functools.partial(states_kernel, mine),
        out_shape=out,
        in_specs=[ANYWHERE] * (4 + len(after)),
        out_specs=[IN_VMEM] * len(out),
        scratch_shapes=[pltpu.SemaphoreType.DMA((HALF // READS, 4))],
        compiler_params=pltpu.CompilerParams(vmem_limit_bytes=2 << 20),
        cost_estimate=CHEAP,
        name="states",
    )(*sources, *after)
    return local, sums, (early, late)


def within_kernel(scale, q, k, v, o, *rest):
    dq, dk, dv = rest[-3:]
    rows = q.shape[0]
    at_row = lax.broadcasted_iota(jnp.int32, (SUB, SUB), 0)
    at_column = lax.broadcasted_iota(jnp.int32, (SUB, SUB), 1)
    lower = at_row >= at_column
    upper = at_row <= at_column
    for head in range(HALF):
        at = pl.ds(head * HEAD_DIM, HEAD_DIM)
        for sub in range(rows // SUB):
            span = pl.ds(sub * SUB, SUB)
            q_one, k_one, v_one, o_one = q[span, at], k[span, at], v[span, at], o[span, at]
            weights = jnp.where(upper, scale * dot(k_one, q_one, NT), 0.0).astype(jnp.bfloat16)
            grads = jnp.where(lower, scale * dot(o_one, v_one, NT), 0.0).astype(jnp.bfloat16)
            grads_t = jnp.where(upper, scale * dot(v_one, o_one, NT), 0.0).astype(jnp.bfloat16)
            dq[span, at] = dot(grads, k_one, NN).astype(PARTIAL)
            dk[span, at] = dot(grads_t, q_one, NN).astype(PARTIAL)
            dv[span, at] = dot(weights, o_one, NN).astype(PARTIAL)


def within(scale, local, after):
    rows = local[0].shape[0]
    return pl.pallas_call(
        functools.partial(within_kernel, scale),
        out_shape=[pltpu.VMEM((rows, COLUMNS), PARTIAL)] * 3,
        in_specs=[IN_VMEM] * 4 + [ANYWHERE] * len(after),
        out_specs=[IN_VMEM] * 3,
        compiler_params=pltpu.CompilerParams(vmem_limit_bytes=2 << 20),
        cost_estimate=CHEAP,
        name="within",
    )(*local, *after)


def join_kernel(turns, sums, sums_in, *sent):
    earlier = [comes_earlier(turn) for turn in turns]
    for index, (start, stop) in enumerate(CHUNKS):
        for head in range(start, stop):
            forward = sums[0, head] + sums_in[0, head]
            backward = sums[1, head] + sums_in[1, head]
            for i in range(len(turns)):
                sent[index * len(turns) + i][head - start] = jnp.where(earlier[i], backward, forward)


def join(turns, sums, sums_in):
    out = [
        pltpu.VMEM((stop - start, HEAD_DIM, HEAD_DIM), jnp.float32) for start, stop in CHUNKS for _ in turns
    ]
    return pl.pallas_call(
        functools.partial(join_kernel, turns),
        out_shape=out,
        in_specs=[IN_VMEM] * 2,
        out_specs=[IN_VMEM] * len(out),
        compiler_params=pltpu.CompilerParams(vmem_limit_bytes=2 << 20),
        cost_estimate=CHEAP,
        name="join",
    )(sums, sums_in)


def combine_kernel(turns, start, *refs):
    received, (sums, sums_in) = refs[: len(turns)], refs[len(turns) : len(turns) + 2]
    own, other = refs[-2:]
    second = my_core() == 1
    earlier = [comes_earlier(turn) for turn in turns]
    for head in range(own.shape[1]):
        prefix = jnp.zeros((HEAD_DIM, HEAD_DIM), jnp.float32)
        suffix = jnp.zeros((HEAD_DIM, HEAD_DIM), jnp.float32)
        for i in range(len(turns)):
            value = received[i][head]
            prefix = prefix + jnp.where(earlier[i], value, 0.0)
            suffix = suffix + jnp.where(earlier[i], 0.0, value)
        own[0, head] = prefix + jnp.where(second, sums_in[0, start + head], 0.0)
        own[1, head] = suffix + jnp.where(second, 0.0, sums_in[1, start + head])
        other[0, head] = prefix + jnp.where(second, 0.0, sums[0, start + head])
        other[1, head] = suffix + jnp.where(second, sums[1, start + head], 0.0)


def combine(turns, chunk, received, sums, sums_in, after):
    start, stop = chunk
    return pl.pallas_call(
        functools.partial(combine_kernel, turns, start),
        out_shape=[state_of(stop - start)] * 2,
        in_specs=[IN_VMEM] * (len(received) + 2) + [ANYWHERE] * len(after),
        out_specs=[IN_VMEM] * 2,
        compiler_params=pltpu.CompilerParams(vmem_limit_bytes=3 << 20),
        cost_estimate=CHEAP,
        name="combine",
    )(*received, sums, sums_in, *after)


def finish_kernel(scale, mine, chunk, k, v, o, dq, dk, dv, state, early, late, *rest):
    *targets, dq_out, dk_out, dv_out, sems = rest[-7:]
    rows = k.shape[0]
    subs = rows // SUB
    first, stop = chunk
    base = half_start(mine)
    width = 2 * HEAD_DIM
    copies = []
    for head in range(first, stop):
        at = pl.ds(head * HEAD_DIM, HEAD_DIM)
        to = pl.ds((head - first) * HEAD_DIM, HEAD_DIM)
        for sub in range(subs):
            span = pl.ds(sub * SUB, SUB)
            before, later = state[0, head - first], state[1, head - first]
            if sub > 0:
                before = before + early[head, sub - 1]
            if sub < subs - 1:
                later = later + late[head, sub]
            before, later = before.astype(jnp.bfloat16), later.astype(jnp.bfloat16)
            dq_out[span, to] = (dq[span, at] + scale * dot(o[span, at], before, NT)).astype(jnp.bfloat16)
            dk_out[span, to] = (dk[span, at] + scale * dot(v[span, at], later, NT)).astype(jnp.bfloat16)
            dv_out[span, to] = (dv[span, at] + scale * dot(k[span, at], later, NN)).astype(jnp.bfloat16)
        if (head - first) % 2 == 1:
            done = (head - 1) * HEAD_DIM
            for i, (source, target) in enumerate(zip((dq_out, dk_out, dv_out), targets, strict=True)):
                copy = pltpu.make_async_copy(
                    source.at[:, pl.ds(done - first * HEAD_DIM, width)],
                    target.at[:, pl.ds(pl.multiple_of(base + done, width), width)],
                    sems.at[(head - first) // 2, i],
                )
                copy.start()
                copies.append(copy)
    for copy in copies:
        copy.wait()


def finish(scale, mine, chunk, local, partials, state, inner, before):
    rows = local[0].shape[0]
    heads = chunk[1] - chunk[0]
    out = [jax.ShapeDtypeStruct((rows, HEADS * HEAD_DIM), jnp.bfloat16)] * 3
    operands = [*local[1:], *partials, state, *inner, *before]
    return pl.pallas_call(
        functools.partial(finish_kernel, scale, mine, chunk),
        out_shape=out,
        in_specs=[IN_VMEM] * 9 + [ANYWHERE] * len(before),
        out_specs=[ANYWHERE] * 3,
        scratch_shapes=[pltpu.VMEM((rows, heads * HEAD_DIM), jnp.bfloat16)] * 3
        + [pltpu.SemaphoreType.DMA((heads // 2, 3))],
        input_output_aliases={9 + i: i for i in range(len(before))},
        compiler_params=pltpu.CompilerParams(vmem_limit_bytes=5 << 20),
        cost_estimate=LONG,
        name="finish",
    )(*operands)


def on_device(queries, key_rows, value_rows, out_grad):
    count = lax.axis_size("seq")
    scale = (HEAD_DIM * queries.shape[0] * count) ** -0.5
    turns = range(1, count // 2)
    sources = [
        pltpu.with_memory_space_constraint(array, pltpu.HBM) for array in (queries, key_rows, value_rows, out_grad)
    ]

    def swap(value):
        return lax.ppermute(value, "seq", [(i, i ^ 1) for i in range(count)])

    local_b, sums_b, inner_b = states(False, sources, ())
    sums_in = swap(sums_b)
    local_a, sums_a, inner_a = states(True, sources, (sums_b,))
    sent = join(turns, sums_a, sums_in)
    received = [
        lax.ppermute(value, "seq", [(i, i ^ (2 * turns[n % len(turns)])) for i in range(count)])
        for n, value in enumerate(sent)
    ]
    partials_b = within(scale, local_b, sent)
    partials_a = within(scale, local_a, (partials_b[0],))
    done = ()
    after = (partials_a[0],)
    for index, chunk in enumerate(CHUNKS):
        values = received[index * len(turns) : (index + 1) * len(turns)]
        own, other = combine(turns, chunk, values, sums_a, sums_in, after)
        other = swap(other)
        done = finish(scale, True, chunk, local_a, partials_a, own, inner_a, done)
        done = finish(scale, False, chunk, local_b, partials_b, other, inner_b, done)
        after = (pltpu.with_memory_space_constraint(done[0], pltpu.HBM),)
    return tuple(done)


def solution(mesh):
    placed = P(("lists", "seq"), None)
    return jax.shard_map(
        on_device,
        mesh=mesh,
        in_specs=(placed,) * 4,
        out_specs=(placed,) * 3,
        check_vma=False,
    )
```

```python
import functools

import jax
import jax.numpy as jnp
from jax import lax
from jax.experimental import pallas as pl
from jax.experimental.pallas import tpu as pltpu
from jax.sharding import PartitionSpec as P

HEADS = 16
HEAD_DIM = 128
HALF = HEADS // 2
COLUMNS = HALF * HEAD_DIM
CHUNKS = ((0, 4), (4, 8))
SUB = 256
PARTIAL = jnp.float32

TN = (((0,), (0,)), ((), ()))
NT = (((1,), (1,)), ((), ()))
NN = (((1,), (0,)), ((), ()))

IN_VMEM = pl.BlockSpec(memory_space=pltpu.VMEM)
ANYWHERE = pl.BlockSpec(memory_space=pl.ANY)
SHORT = pl.CostEstimate(flops=1000, bytes_accessed=1000, transcendentals=0)
LONG = pl.CostEstimate(flops=2 * 10**10, bytes_accessed=1000, transcendentals=0)


def dot(left, right, dims):
    return lax.dot_general(left, right, dims, preferred_element_type=jnp.float32)


def heads_of(chunk):
    return chunk[1] - chunk[0]


def state_of(heads):
    return pltpu.VMEM((2, heads, HEAD_DIM, HEAD_DIM), jnp.float32)


def head_columns(head):
    return pl.ds(head * HEAD_DIM, HEAD_DIM)


def my_core():
    return lax.rem(lax.axis_index("seq"), 2)


def comes_earlier(turn):
    pair = lax.div(lax.axis_index("seq"), 2)
    return jnp.bitwise_xor(pair, turn) < pair


def first_column(mine, chunk):
    half = my_core() if mine else 1 - my_core()
    return half * COLUMNS + chunk[0] * HEAD_DIM


def call(kernel, out, operands, after=(), scratch=(), cost=SHORT, limit=3, name=None):
    return pl.pallas_call(
        kernel,
        out_shape=out,
        in_specs=[IN_VMEM] * len(operands) + [ANYWHERE] * len(after),
        out_specs=[IN_VMEM] * len(out),
        scratch_shapes=list(scratch),
        compiler_params=pltpu.CompilerParams(vmem_limit_bytes=limit << 20),
        cost_estimate=cost,
        name=name,
    )(*operands, *after)


def read(mine, chunk, sources, local, sems):
    width = heads_of(chunk) * HEAD_DIM
    at = pl.ds(pl.multiple_of(first_column(mine, chunk), HEAD_DIM), width)
    copies = []
    for i in (1, 2, 0, 3):
        copy = pltpu.make_async_copy(sources[i].at[:, at], local[i], sems.at[i])
        copy.start()
        copies.append(copy)
    return copies


def sum_up(copies, local, sums, early, late):
    q, k, v, o = local
    subs = q.shape[0] // SUB
    for kind, (left, right) in enumerate(((k, v), (q, o))):
        copies[2 * kind].wait()
        copies[2 * kind + 1].wait()
        order = list(range(subs)) if kind == 0 else list(range(subs - 1, -1, -1))
        for head in range(sums.shape[1]):
            at = head_columns(head)
            total = None
            for sub in order:
                span = pl.ds(sub * SUB, SUB)
                part = dot(left[span, at], right[span, at], TN)
                total = part if total is None else total + part
                if sub != order[-1]:
                    if kind == 0:
                        early[head, sub] = total
                    else:
                        late[head, sub - 1] = total
            sums[kind, head] = total


def work_inside(scale, local, outs):
    (q, k, v, o), (dq, dk, dv) = local, outs
    rows, columns = q.shape
    at_row = lax.broadcasted_iota(jnp.int32, (SUB, SUB), 0)
    at_column = lax.broadcasted_iota(jnp.int32, (SUB, SUB), 1)
    lower = at_row >= at_column
    upper = at_row <= at_column

    def weights_of(unit):
        head, sub = unit
        at, span = head_columns(head), pl.ds(sub * SUB, SUB)
        q_one, k_one, v_one, o_one = q[span, at], k[span, at], v[span, at], o[span, at]
        return (
            jnp.where(lower, scale * dot(o_one, v_one, NT), 0.0).astype(jnp.bfloat16),
            jnp.where(upper, scale * dot(v_one, o_one, NT), 0.0).astype(jnp.bfloat16),
            jnp.where(upper, scale * dot(k_one, q_one, NT), 0.0).astype(jnp.bfloat16),
        )

    units = [(head, sub) for head in range(columns // HEAD_DIM) for sub in range(rows // SUB)]
    ahead = weights_of(units[0])
    for number, (head, sub) in enumerate(units):
        grads, grads_t, weights = ahead
        if number + 1 < len(units):
            ahead = weights_of(units[number + 1])
        at, span = head_columns(head), pl.ds(sub * SUB, SUB)
        dq[span, at] = dot(grads, k[span, at], NN).astype(PARTIAL)
        dk[span, at] = dot(grads_t, q[span, at], NN).astype(PARTIAL)
        dv[span, at] = dot(weights, o[span, at], NN).astype(PARTIAL)


def shapes_of(rows, chunk):
    heads = heads_of(chunk)
    local = [pltpu.VMEM((rows, heads * HEAD_DIM), jnp.bfloat16)] * 4
    inner = pltpu.VMEM((heads, rows // SUB - 1, HEAD_DIM, HEAD_DIM), jnp.float32)
    partials = [pltpu.VMEM((rows, heads * HEAD_DIM), PARTIAL)] * 3
    return local, [state_of(heads), inner, inner], partials


def states_kernel(mine, chunk, *refs):
    sources, local, sums, sems = refs[:4], refs[-8:-4], refs[-4:-1], refs[-1]
    sum_up(read(mine, chunk, sources, local, sems), local, *sums)


def states(mine, chunk, sources, after):
    local, sums, _ = shapes_of(sources[0].shape[0], chunk)
    result = pl.pallas_call(
        functools.partial(states_kernel, mine, chunk),
        out_shape=local + sums,
        in_specs=[ANYWHERE] * (4 + len(after)),
        out_specs=[IN_VMEM] * 7,
        scratch_shapes=[pltpu.SemaphoreType.DMA((4,))],
        compiler_params=pltpu.CompilerParams(vmem_limit_bytes=2 << 20),
        cost_estimate=LONG,
        name="states",
    )(*sources, *after)
    return result[:4], result[4], result[5:]


def states_both_kernel(chunk, *refs):
    sources, parts, sems = refs[:4], (refs[-15:-8], refs[-8:-1]), refs[-1]
    copies = [read(bool(mine), chunk, sources, parts[mine][:4], sems.at[mine]) for mine in range(2)]
    for mine in range(2):
        sum_up(copies[mine], parts[mine][:4], *parts[mine][4:])


def states_both(chunk, sources, after):
    local, sums, _ = shapes_of(sources[0].shape[0], chunk)
    result = pl.pallas_call(
        functools.partial(states_both_kernel, chunk),
        out_shape=(local + sums) * 2,
        in_specs=[ANYWHERE] * (4 + len(after)),
        out_specs=[IN_VMEM] * 14,
        scratch_shapes=[pltpu.SemaphoreType.DMA((2, 4))],
        compiler_params=pltpu.CompilerParams(vmem_limit_bytes=2 << 20),
        cost_estimate=LONG,
        name="states_both",
    )(*sources, *after)
    return [(part[:4], part[4], part[5:]) for part in (result[:7], result[7:])]


def within_kernel(scale, *refs):
    work_inside(scale, refs[:4], refs[-3:])


def within(scale, chunk, local, after):
    partials = shapes_of(local[0].shape[0], chunk)[2]
    return call(functools.partial(within_kernel, scale), partials, local, after, cost=LONG, name="within")


def join_kernel(turns, sums, sums_in, *rest):
    sent = rest[-len(turns) :]
    for head in range(sums.shape[1]):
        forward = sums[0, head] + sums_in[0, head]
        backward = sums[1, head] + sums_in[1, head]
        for turn, out in zip(turns, sent, strict=True):
            out[head] = jnp.where(comes_earlier(turn), backward, forward)


def join(turns, sums, sums_in, after):
    out = [pltpu.VMEM(sums.shape[1:], jnp.float32)] * len(turns)
    return call(functools.partial(join_kernel, turns), out, (sums, sums_in), after, name="join")


def combine_kernel(turns, *refs):
    received, (sums, sums_in) = refs[: len(turns)], refs[len(turns) : len(turns) + 2]
    own, other = refs[-2:]
    second = my_core() == 1
    for head in range(sums.shape[1]):
        prefix = jnp.zeros((HEAD_DIM, HEAD_DIM), jnp.float32)
        suffix = jnp.zeros((HEAD_DIM, HEAD_DIM), jnp.float32)
        for turn, value in zip(turns, received, strict=True):
            earlier = comes_earlier(turn)
            prefix = prefix + jnp.where(earlier, value[head], 0.0)
            suffix = suffix + jnp.where(earlier, 0.0, value[head])
        own[0, head] = prefix + jnp.where(second, sums_in[0, head], 0.0)
        own[1, head] = suffix + jnp.where(second, 0.0, sums_in[1, head])
        other[0, head] = prefix + jnp.where(second, 0.0, sums[0, head])
        other[1, head] = suffix + jnp.where(second, sums[1, head], 0.0)


def combine(turns, received, sums, sums_in, after):
    out = [state_of(sums.shape[1])] * 2
    return call(functools.partial(combine_kernel, turns), out, (*received, sums, sums_in), after, name="combine")


def finish_kernel(scale, chunk, halves, *refs):
    targets, staged, sems = refs[-7:-4], refs[-4:-1], refs[-1]
    heads = heads_of(chunk)
    copies = []
    for number, mine in enumerate(halves):
        k, v, o, dq, dk, dv, state, early, late = refs[9 * number : 9 * number + 9]
        rows = k.shape[0]
        subs = rows // SUB
        base = first_column(mine, chunk)
        for head in range(heads):
            at = head_columns(head)
            to = head_columns(number * heads + head)
            for sub in range(subs):
                span = pl.ds(sub * SUB, SUB)
                before, later = state[0, head], state[1, head]
                if sub > 0:
                    before = before + early[head, sub - 1]
                if sub < subs - 1:
                    later = later + late[head, sub]
                before, later = before.astype(jnp.bfloat16), later.astype(jnp.bfloat16)
                pieces = (
                    dq[span, at] + scale * dot(o[span, at], before, NT),
                    dk[span, at] + scale * dot(v[span, at], later, NT),
                    dv[span, at] + scale * dot(k[span, at], later, NN),
                )
                for out, piece in zip(staged, pieces, strict=True):
                    out[span, to] = piece.astype(jnp.bfloat16)
            if head % 2 == 1 or head == heads - 1:
                first, width = (head - head % 2) * HEAD_DIM, (1 + head % 2) * HEAD_DIM
                for i in range(3):
                    copy = pltpu.make_async_copy(
                        staged[i].at[:, pl.ds(number * heads * HEAD_DIM + first, width)],
                        targets[i].at[:, pl.ds(pl.multiple_of(base + first, HEAD_DIM), width)],
                        sems.at[number, head // 2, i],
                    )
                    copy.start()
                    copies.append(copy)
    for copy in copies:
        copy.wait()


def finish(scale, chunk, parts, before):
    rows = parts[0][1][0].shape[0]
    out = [jax.ShapeDtypeStruct((rows, HEADS * HEAD_DIM), jnp.bfloat16)] * 3
    halves = tuple(part[0] for part in parts)
    operands = []
    for _, local, partials, state, inner in parts:
        operands += [*local[1:], *partials, state, *inner]
    width = len(parts) * heads_of(chunk) * HEAD_DIM
    return pl.pallas_call(
        functools.partial(finish_kernel, scale, chunk, halves),
        out_shape=out,
        in_specs=[IN_VMEM] * len(operands) + [ANYWHERE] * len(before),
        out_specs=[ANYWHERE] * 3,
        scratch_shapes=[pltpu.VMEM((rows, width), jnp.bfloat16)] * 3
        + [pltpu.SemaphoreType.DMA((len(parts), (heads_of(chunk) + 1) // 2, 3))],
        input_output_aliases={len(operands) + i: i for i in range(len(before))},
        compiler_params=pltpu.CompilerParams(vmem_limit_bytes=(2 + 3 * len(parts)) << 20),
        cost_estimate=LONG,
        name="finish",
    )(*operands, *before)


def on_device(queries, key_rows, value_rows, out_grad):
    count = lax.axis_size("seq")
    scale = (HEAD_DIM * queries.shape[0] * count) ** -0.5
    turns = range(1, count // 2)
    sources = [
        pltpu.with_memory_space_constraint(array, pltpu.HBM) for array in (queries, key_rows, value_rows, out_grad)
    ]
    early_chunk, late_chunk = CHUNKS

    def trade(value, distance):
        return lax.ppermute(value, "seq", [(i, i ^ distance) for i in range(count)])

    def trade_all(values):
        return [trade(value, 2 * turn) for turn, value in zip(turns, values, strict=True)]

    local_eo, sums_eo, inner_eo = states(False, early_chunk, sources, ())
    sums_e_in = trade(sums_eo, 1)
    local_em, sums_em, inner_em = states(True, early_chunk, sources, (sums_eo,))
    sent_e = join(turns, sums_em, sums_e_in, ())
    received_e = trade_all(sent_e)

    (local_lo, sums_lo, inner_lo), (local_lm, sums_lm, inner_lm) = states_both(late_chunk, sources, sent_e)
    sums_l_in = trade(sums_lo, 1)
    partials_eo = within(scale, early_chunk, local_eo, (sums_lo,))
    sent_l = join(turns, sums_lm, sums_l_in, (partials_eo[0],))
    received_l = trade_all(sent_l)
    partials_em = within(scale, early_chunk, local_em, (received_e[0], *sent_l))
    partials_lo = within(scale, late_chunk, local_lo, (partials_em[0],))

    own_e, other_e = combine(turns, received_e, sums_em, sums_e_in, (partials_lo[0],))
    other_e = trade(other_e, 1)
    partials_lm = within(scale, late_chunk, local_lm, (own_e,))
    done = finish(
        scale,
        early_chunk,
        [(True, local_em, partials_em, own_e, inner_em), (False, local_eo, partials_eo, other_e, inner_eo)],
        (),
    )

    held_back = (pltpu.with_memory_space_constraint(done[0], pltpu.HBM), partials_lm[0])
    own_l, other_l = combine(turns, received_l, sums_lm, sums_l_in, held_back)
    other_l = trade(other_l, 1)
    done = finish(scale, late_chunk, [(True, local_lm, partials_lm, own_l, inner_lm)], done)
    return tuple(finish(scale, late_chunk, [(False, local_lo, partials_lo, other_l, inner_lo)], done))


def solution(mesh):
    placed = P(("lists", "seq"), None)
    return jax.shard_map(
        on_device,
        mesh=mesh,
        in_specs=(placed,) * 4,
        out_specs=(placed,) * 3,
        check_vma=False,
    )
```

```python
import functools

import jax
import jax.numpy as jnp
from jax import lax
from jax.experimental import pallas as pl
from jax.experimental.pallas import tpu as pltpu
from jax.sharding import PartitionSpec as P

HEADS = 16
HEAD_DIM = 128
HALF = HEADS // 2
COLUMNS = HALF * HEAD_DIM
GROUP = HALF // 2
SUB = 256
PARTIAL = jnp.float32

TN = (((0,), (0,)), ((), ()))
NT = (((1,), (1,)), ((), ()))
NN = (((1,), (0,)), ((), ()))

IN_VMEM = pl.BlockSpec(memory_space=pltpu.VMEM)
ANYWHERE = pl.BlockSpec(memory_space=pl.ANY)
SHORT = pl.CostEstimate(flops=1000, bytes_accessed=1000, transcendentals=0)
LONG = pl.CostEstimate(flops=2 * 10**10, bytes_accessed=1000, transcendentals=0)


def dot(left, right, dims):
    return lax.dot_general(left, right, dims, preferred_element_type=jnp.float32)


def state_of(heads):
    return pltpu.VMEM((2, heads, HEAD_DIM, HEAD_DIM), jnp.float32)


def head_columns(head):
    return pl.ds(head * HEAD_DIM, HEAD_DIM)


def my_core():
    return lax.rem(lax.axis_index("seq"), 2)


def my_pair():
    return lax.div(lax.axis_index("seq"), 2)


def first_column(square, mine, group):
    half = my_core() if mine else 1 - my_core()
    if square:
        pair = my_pair()
        group = jnp.where((pair == 1) | (pair == 2), 1 - group, group)
    return half * COLUMNS + group * (GROUP * HEAD_DIM)


def call(kernel, out, operands, after=(), scratch=(), cost=SHORT, limit=3, name=None):
    return pl.pallas_call(
        kernel,
        out_shape=out,
        in_specs=[IN_VMEM] * len(operands) + [ANYWHERE] * len(after),
        out_specs=[IN_VMEM] * len(out),
        scratch_shapes=list(scratch),
        compiler_params=pltpu.CompilerParams(vmem_limit_bytes=limit << 20),
        cost_estimate=cost,
        name=name,
    )(*operands, *after)


def read(square, mine, group, sources, local, sems):
    width = GROUP * HEAD_DIM
    at = pl.ds(pl.multiple_of(first_column(square, mine, group), width), width)
    copies = []
    for i in (1, 2, 0, 3):
        copy = pltpu.make_async_copy(sources[i].at[:, at], local[i], sems.at[i])
        copy.start()
        copies.append(copy)
    return copies


def sum_up(copies, local, sums, early, late):
    q, k, v, o = local
    subs = q.shape[0] // SUB
    for kind, (left, right) in enumerate(((k, v), (q, o))):
        copies[2 * kind].wait()
        copies[2 * kind + 1].wait()
        order = list(range(subs)) if kind == 0 else list(range(subs - 1, -1, -1))
        for head in range(sums.shape[1]):
            at = head_columns(head)
            total = None
            for sub in order:
                span = pl.ds(sub * SUB, SUB)
                part = dot(left[span, at], right[span, at], TN)
                total = part if total is None else total + part
                if sub != order[-1]:
                    if kind == 0:
                        early[head, sub] = total
                    else:
                        late[head, sub - 1] = total
            sums[kind, head] = total


def work_inside(scale, local, outs):
    (q, k, v, o), (dq, dk, dv) = local, outs
    rows, columns = q.shape
    part = SUB // 2
    at_row = lax.broadcasted_iota(jnp.int32, (SUB, SUB), 0)
    at_column = lax.broadcasted_iota(jnp.int32, (SUB, SUB), 1)
    lower = at_row >= at_column
    upper = at_row <= at_column
    nothing = jnp.zeros((part, HEAD_DIM), jnp.bfloat16)

    def weights_of(unit):
        pair, sub = unit
        span = pl.ds(sub * SUB, SUB)
        weights = []
        for head in (2 * pair, 2 * pair + 1):
            at = head_columns(head)
            grads = jnp.where(lower, scale * dot(o[span, at], v[span, at], NT), 0.0).astype(jnp.bfloat16)
            forward = jnp.where(upper, scale * dot(k[span, at], q[span, at], NT), 0.0).astype(jnp.bfloat16)
            weights.append((grads, grads.T, forward))
        return weights

    def side_by_side(weights, rows):
        left = jnp.concatenate([rows[0], nothing], axis=1)
        right = jnp.concatenate([nothing, rows[1]], axis=1)
        product = dot(jnp.concatenate(weights, axis=1), jnp.concatenate([left, right], axis=0), NN)
        return product[:, :HEAD_DIM], product[:, HEAD_DIM:]

    def lower_product(weights, rows):
        first = side_by_side([w[:part, :part] for w in weights], [r[:part] for r in rows])
        return [
            jnp.concatenate([top, dot(w[part:], r, NN)], axis=0) for top, w, r in zip(first, weights, rows, strict=True)
        ]

    def upper_product(weights, rows):
        last = side_by_side([w[part:, part:] for w in weights], [r[part:] for r in rows])
        return [
            jnp.concatenate([dot(w[:part], r, NN), below], axis=0) for below, w, r in zip(last, weights, rows, strict=True)
        ]

    units = [(pair, sub) for pair in range(columns // HEAD_DIM // 2) for sub in range(rows // SUB)]
    ahead = weights_of(units[0])
    for number, (pair, sub) in enumerate(units):
        grads, grads_t, forward = zip(*ahead, strict=True)
        if number + 1 < len(units):
            ahead = weights_of(units[number + 1])
        span = pl.ds(sub * SUB, SUB)
        places = [head_columns(2 * pair), head_columns(2 * pair + 1)]
        for product, weights, source, out in (
            (lower_product, grads, k, dq),
            (upper_product, grads_t, q, dk),
            (upper_product, forward, o, dv),
        ):
            for at, piece in zip(places, product(weights, [source[span, at] for at in places]), strict=True):
                out[span, at] = piece.astype(PARTIAL)


def shapes_of(rows):
    heads = GROUP
    local = [pltpu.VMEM((rows, heads * HEAD_DIM), jnp.bfloat16)] * 4
    inner = pltpu.VMEM((heads, rows // SUB - 1, HEAD_DIM, HEAD_DIM), jnp.float32)
    partials = [pltpu.VMEM((rows, heads * HEAD_DIM), PARTIAL)] * 3
    return local, [state_of(heads), inner, inner], partials


def states_kernel(square, mine, group, *refs):
    sources, local, sums, sems = refs[:4], refs[-8:-4], refs[-4:-1], refs[-1]
    sum_up(read(square, mine, group, sources, local, sems), local, *sums)


def states(square, mine, group, sources, after):
    local, sums, _ = shapes_of(sources[0].shape[0])
    result = pl.pallas_call(
        functools.partial(states_kernel, square, mine, group),
        out_shape=local + sums,
        in_specs=[ANYWHERE] * (4 + len(after)),
        out_specs=[IN_VMEM] * 7,
        scratch_shapes=[pltpu.SemaphoreType.DMA((4,))],
        compiler_params=pltpu.CompilerParams(vmem_limit_bytes=2 << 20),
        cost_estimate=LONG,
        name="states",
    )(*sources, *after)
    return result[:4], result[4], result[5:]


def states_both_kernel(square, group, *refs):
    sources, parts, sems = refs[:4], (refs[-15:-8], refs[-8:-1]), refs[-1]
    copies = [read(square, bool(mine), group, sources, parts[mine][:4], sems.at[mine]) for mine in range(2)]
    for mine in range(2):
        sum_up(copies[mine], parts[mine][:4], *parts[mine][4:])


def states_both(square, group, sources, after):
    local, sums, _ = shapes_of(sources[0].shape[0])
    result = pl.pallas_call(
        functools.partial(states_both_kernel, square, group),
        out_shape=(local + sums) * 2,
        in_specs=[ANYWHERE] * (4 + len(after)),
        out_specs=[IN_VMEM] * 14,
        scratch_shapes=[pltpu.SemaphoreType.DMA((2, 4))],
        compiler_params=pltpu.CompilerParams(vmem_limit_bytes=2 << 20),
        cost_estimate=LONG,
        name="states_both",
    )(*sources, *after)
    return [(part[:4], part[4], part[5:]) for part in (result[:7], result[7:])]


def within_kernel(scale, *refs):
    work_inside(scale, refs[:4], refs[-3:])


def within(scale, local, after):
    partials = shapes_of(local[0].shape[0])[2]
    return call(functools.partial(within_kernel, scale), partials, local, after, cost=LONG, name="within")


def settle(head, prefix, suffix, sums, sums_in, own, other):
    second = my_core() == 1
    own[0, head] = prefix + jnp.where(second, sums_in[0, head], 0.0)
    own[1, head] = suffix + jnp.where(second, 0.0, sums_in[1, head])
    other[0, head] = prefix + jnp.where(second, 0.0, sums[0, head])
    other[1, head] = suffix + jnp.where(second, sums[1, head], 0.0)


PIECE = pltpu.VMEM((GROUP, HEAD_DIM, HEAD_DIM), jnp.float32)
STATES = [state_of(GROUP)] * 2


def comes_earlier(turn):
    pair = my_pair()
    return jnp.bitwise_xor(pair, turn) < pair


def join_kernel(turns, sums, sums_in, *rest):
    sent = rest[-len(turns) :]
    for head in range(GROUP):
        forward = sums[0, head] + sums_in[0, head]
        backward = sums[1, head] + sums_in[1, head]
        for turn, out in zip(turns, sent, strict=True):
            out[head] = jnp.where(comes_earlier(turn), backward, forward)


def combine_kernel(turns, *refs):
    received, (sums, sums_in) = refs[: len(turns)], refs[len(turns) : len(turns) + 2]
    for head in range(GROUP):
        prefix = jnp.zeros((HEAD_DIM, HEAD_DIM), jnp.float32)
        suffix = jnp.zeros((HEAD_DIM, HEAD_DIM), jnp.float32)
        for turn, value in zip(turns, received, strict=True):
            earlier = comes_earlier(turn)
            prefix = prefix + jnp.where(earlier, value[head], 0.0)
            suffix = suffix + jnp.where(earlier, 0.0, value[head])
        settle(head, prefix, suffix, sums, sums_in, *refs[-2:])


def row_first_kernel(sums, sums_in, *rest):
    lower = lax.div(my_pair(), 2)
    for head in range(GROUP):
        rest[-1][head] = sums[lower, head] + sums_in[lower, head]


def row_second_kernel(sums, sums_in, *rest):
    right = lax.rem(my_pair(), 2)
    for head in range(GROUP):
        rest[-1][head] = sums[right, head] + sums_in[right, head]


def column_kernel(sums, sums_in, from_row, *rest):
    lower = lax.div(my_pair(), 2)
    for head in range(GROUP):
        rest[-1][head] = sums[lower, head] + sums_in[lower, head] + from_row[head]


def row_third_kernel(sums, sums_in, from_column, *rest):
    pair = my_pair()
    outer = (pair == 0) | (pair == 3)
    kind = jnp.where(pair == 1, 1, 0)
    for head in range(GROUP):
        rest[-1][head] = jnp.where(outer, from_column[head], sums[kind, head] + sums_in[kind, head])


def first_states_kernel(sums, sums_in, row_second, column_first, *rest):
    pair = my_pair()
    below, right = pair >= 2, lax.rem(pair, 2) == 1
    for head in range(GROUP):
        row, column = row_second[head], column_first[head]
        prefix = jnp.where(right, row, 0.0) + jnp.where(below, column, 0.0)
        suffix = jnp.where(right, 0.0, row) + jnp.where(below, 0.0, column)
        settle(head, prefix, suffix, sums, sums_in, *rest[-2:])


def second_states_kernel(sums, sums_in, row_first, row_third, column_second, *rest):
    pair = my_pair()
    below, outer = pair >= 2, (pair == 0) | (pair == 3)
    for head in range(GROUP):
        passed = row_third[head] + jnp.where(outer, column_second[head], 0.0)
        prefix = jnp.where(pair == 1, row_first[head], 0.0) + jnp.where(below, passed, 0.0)
        suffix = jnp.where(pair == 2, row_first[head], 0.0) + jnp.where(below, 0.0, passed)
        settle(head, prefix, suffix, sums, sums_in, *rest[-2:])


def finish_kernel(scale, square, group, halves, *refs):
    targets, staged, sems = refs[-7:-4], refs[-4:-1], refs[-1]
    heads = GROUP
    copies = []
    for number, mine in enumerate(halves):
        k, v, o, dq, dk, dv, state, early, late = refs[9 * number : 9 * number + 9]
        rows = k.shape[0]
        subs = rows // SUB
        base = first_column(square, mine, group)
        for head in range(heads):
            at = head_columns(head)
            to = head_columns(number * heads + head)
            for sub in range(subs):
                span = pl.ds(sub * SUB, SUB)
                before, later = state[0, head], state[1, head]
                if sub > 0:
                    before = before + early[head, sub - 1]
                if sub < subs - 1:
                    later = later + late[head, sub]
                before, later = before.astype(jnp.bfloat16), later.astype(jnp.bfloat16)
                pieces = (
                    dq[span, at] + scale * dot(o[span, at], before, NT),
                    dk[span, at] + scale * dot(v[span, at], later, NT),
                    dv[span, at] + scale * dot(k[span, at], later, NN),
                )
                for out, piece in zip(staged, pieces, strict=True):
                    out[span, to] = piece.astype(jnp.bfloat16)
            if head % 2 == 1 or head == heads - 1:
                first, width = (head - head % 2) * HEAD_DIM, (1 + head % 2) * HEAD_DIM
                for i in range(3):
                    copy = pltpu.make_async_copy(
                        staged[i].at[:, pl.ds(number * heads * HEAD_DIM + first, width)],
                        targets[i].at[:, pl.ds(pl.multiple_of(base + first, HEAD_DIM), width)],
                        sems.at[number, head // 2, i],
                    )
                    copy.start()
                    copies.append(copy)
    for copy in copies:
        copy.wait()


def finish(scale, square, group, parts, before):
    rows = parts[0][1][0].shape[0]
    out = [jax.ShapeDtypeStruct((rows, HEADS * HEAD_DIM), jnp.bfloat16)] * 3
    halves = tuple(part[0] for part in parts)
    operands = []
    for _, local, partials, state, inner in parts:
        operands += [*local[1:], *partials, state, *inner]
    width = len(parts) * GROUP * HEAD_DIM
    return pl.pallas_call(
        functools.partial(finish_kernel, scale, square, group, halves),
        out_shape=out,
        in_specs=[IN_VMEM] * len(operands) + [ANYWHERE] * len(before),
        out_specs=[ANYWHERE] * 3,
        scratch_shapes=[pltpu.VMEM((rows, width), jnp.bfloat16)] * 3
        + [pltpu.SemaphoreType.DMA((len(parts), (GROUP + 1) // 2, 3))],
        input_output_aliases={len(operands) + i: i for i in range(len(before))},
        compiler_params=pltpu.CompilerParams(vmem_limit_bytes=(2 + 3 * len(parts)) << 20),
        cost_estimate=LONG,
        name="finish",
    )(*operands, *before)


def on_device(queries, key_rows, value_rows, out_grad):
    count = lax.axis_size("seq")
    square = count == 8
    scale = (HEAD_DIM * queries.shape[0] * count) ** -0.5
    sources = [
        pltpu.with_memory_space_constraint(array, pltpu.HBM) for array in (queries, key_rows, value_rows, out_grad)
    ]

    def trade(value, distance):
        return lax.ppermute(value, "seq", [(i, i ^ distance) for i in range(count)])

    def run(kernel, out, operands, after):
        return call(kernel, out, operands, after, name=(kernel.func if hasattr(kernel, "func") else kernel).__name__)

    local_eo, sums_eo, inner_eo = states(square, False, 0, sources, ())
    sums_e_in = trade(sums_eo, 1)
    local_em, sums_em, inner_em = states(square, True, 0, sources, (sums_eo,))
    both_e = (sums_em, sums_e_in)
    if square:
        (sent,) = run(row_first_kernel, [PIECE], both_e, ())
        row_first = trade(sent, 2)
        after = (sent,)
    else:
        turns = range(1, count // 2)
        sent = run(functools.partial(join_kernel, turns), [PIECE] * len(turns), both_e, ())
        received = [trade(value, 2 * turn) for turn, value in zip(turns, sent, strict=True)]
        after = tuple(sent)

    (local_lo, sums_lo, inner_lo), (local_lm, sums_lm, inner_lm) = states_both(square, 1, sources, after)
    sums_l_in = trade(sums_lo, 1)
    both_l = (sums_lm, sums_l_in)
    partials_eo = within(scale, local_eo, (sums_lo,))
    if square:
        (sent,) = run(row_second_kernel, [PIECE], both_l, (partials_eo[0],))
        row_second = trade(sent, 2)
        (sent,) = run(column_kernel, [PIECE], (*both_l, row_first), (sent,))
        column_first = trade(sent, 4)
        partials_em = within(scale, local_em, (sent,))
        partials_lo = within(scale, local_lo, (partials_em[0],))
        (sent,) = run(column_kernel, [PIECE], (*both_e, row_second), (partials_lo[0],))
        column_second = trade(sent, 4)
        (sent,) = run(row_third_kernel, [PIECE], (*both_e, column_first), (sent,))
        row_third = trade(sent, 2)
        own_e, other_e = run(first_states_kernel, STATES, (*both_e, row_second, column_first), (sent,))
    else:
        sent = run(functools.partial(join_kernel, turns), [PIECE] * len(turns), both_l, (partials_eo[0],))
        received_l = [trade(value, 2 * turn) for turn, value in zip(turns, sent, strict=True)]
        partials_em = within(scale, local_em, tuple(sent))
        partials_lo = within(scale, local_lo, (partials_em[0],))
        kernel = functools.partial(combine_kernel, turns)
        own_e, other_e = run(kernel, STATES, (*received, *both_e), (partials_lo[0],))

    other_e = trade(other_e, 1)
    partials_lm = within(scale, local_lm, (own_e,))
    parts = [(True, local_em, partials_em, own_e, inner_em), (False, local_eo, partials_eo, other_e, inner_eo)]
    done = finish(scale, square, 0, parts, ())

    after = (pltpu.with_memory_space_constraint(done[0], pltpu.HBM), partials_lm[0])
    if square:
        arrived = (row_first, row_third, column_second)
        own_l, other_l = run(second_states_kernel, STATES, (*both_l, *arrived), after)
    else:
        own_l, other_l = run(kernel, STATES, (*received_l, *both_l), after)
    other_l = trade(other_l, 1)
    done = finish(scale, square, 1, [(True, local_lm, partials_lm, own_l, inner_lm)], done)
    return tuple(finish(scale, square, 1, [(False, local_lo, partials_lo, other_l, inner_lo)], done))


def solution(mesh):
    placed = P(("lists", "seq"), None)
    return jax.shard_map(
        on_device,
        mesh=mesh,
        in_specs=(placed,) * 4,
        out_specs=(placed,) * 3,
        check_vma=False,
    )
```

```python
import functools

import jax
import jax.numpy as jnp
from jax import lax
from jax.experimental import pallas as pl
from jax.experimental.pallas import tpu as pltpu
from jax.sharding import PartitionSpec as P

HEADS = 16
HEAD_DIM = 128
HALF = HEADS // 2
COLUMNS = HALF * HEAD_DIM
GROUP = HALF // 2
SUB = 256
PARTIAL = jnp.float32

TN = (((0,), (0,)), ((), ()))
NT = (((1,), (1,)), ((), ()))
NN = (((1,), (0,)), ((), ()))

IN_VMEM = pl.BlockSpec(memory_space=pltpu.VMEM)
ANYWHERE = pl.BlockSpec(memory_space=pl.ANY)
SHORT = pl.CostEstimate(flops=1000, bytes_accessed=1000, transcendentals=0)
LONG = pl.CostEstimate(flops=2 * 10**10, bytes_accessed=1000, transcendentals=0)


def dot(left, right, dims):
    return lax.dot_general(left, right, dims, preferred_element_type=jnp.float32)


def state_of(heads):
    return pltpu.VMEM((2, heads, HEAD_DIM, HEAD_DIM), jnp.float32)


def head_columns(head):
    return pl.ds(head * HEAD_DIM, HEAD_DIM)


def my_core():
    return lax.rem(lax.axis_index("seq"), 2)


def my_pair():
    return lax.div(lax.axis_index("seq"), 2)


def first_column(square, mine, group):
    half = my_core() if mine else 1 - my_core()
    if square:
        pair = my_pair()
        group = jnp.where((pair == 1) | (pair == 2), 1 - group, group)
    return half * COLUMNS + group * (GROUP * HEAD_DIM)


def my_row(square):
    return lax.div(my_pair(), 2) if square else jnp.int32(0)


PIECE = pltpu.VMEM((GROUP, HEAD_DIM, HEAD_DIM), jnp.float32)
STATES = [state_of(GROUP)] * 2


def call(kernel, out, operands, after=(), scratch=(), cost=SHORT, limit=3, name=None):
    return pl.pallas_call(
        kernel,
        out_shape=out,
        in_specs=[IN_VMEM] * len(operands) + [ANYWHERE] * len(after),
        out_specs=[IN_VMEM] * len(out),
        scratch_shapes=list(scratch),
        compiler_params=pltpu.CompilerParams(vmem_limit_bytes=limit << 20),
        cost_estimate=cost,
        name=name,
    )(*operands, *after)


KINDS = ((1, 2), (0, 3))


def read(square, mine, group, kind, sources, local, sems):
    width = GROUP * HEAD_DIM
    at = pl.ds(pl.multiple_of(first_column(square, mine, group), width), width)
    return [pltpu.make_async_copy(sources[i].at[:, at], local[i], sems.at[i]) for i in KINDS[kind]]


def start_all(copies):
    for copy in copies:
        copy.start()


def sum_kind(kind, copies, local, sums, early, late):
    for copy in copies:
        copy.wait()
    q, k, v, o = local
    left, right = ((k, v), (q, o))[kind]
    subs = q.shape[0] // SUB
    order = list(range(subs)) if kind == 0 else list(range(subs - 1, -1, -1))
    for head in range(GROUP):
        at = head_columns(head)
        total = None
        for sub in order:
            span = pl.ds(sub * SUB, SUB)
            part = dot(left[span, at], right[span, at], TN)
            total = part if total is None else total + part
            if sub != order[-1]:
                if kind == 0:
                    early[head, sub] = total
                else:
                    late[head, sub - 1] = total
        sums[head] = total


def work_inside(scale, local, outs, pairs):
    (q, k, v, o), (dq, dk, dv) = local, outs
    rows = q.shape[0]
    part = SUB // 2
    at_row = lax.broadcasted_iota(jnp.int32, (SUB, SUB), 0)
    at_column = lax.broadcasted_iota(jnp.int32, (SUB, SUB), 1)
    lower = at_row >= at_column
    upper = at_row <= at_column
    nothing = jnp.zeros((part, HEAD_DIM), jnp.bfloat16)

    def weights_of(unit):
        pair, sub = unit
        span = pl.ds(sub * SUB, SUB)
        weights = []
        for head in (2 * pair, 2 * pair + 1):
            at = head_columns(head)
            grads = jnp.where(lower, scale * dot(o[span, at], v[span, at], NT), 0.0).astype(jnp.bfloat16)
            forward = jnp.where(upper, scale * dot(k[span, at], q[span, at], NT), 0.0).astype(jnp.bfloat16)
            weights.append((grads, grads.T, forward))
        return weights

    def side_by_side(weights, rows):
        left = jnp.concatenate([rows[0], nothing], axis=1)
        right = jnp.concatenate([nothing, rows[1]], axis=1)
        product = dot(jnp.concatenate(weights, axis=1), jnp.concatenate([left, right], axis=0), NN)
        return product[:, :HEAD_DIM], product[:, HEAD_DIM:]

    def lower_product(weights, rows):
        first = side_by_side([w[:part, :part] for w in weights], [r[:part] for r in rows])
        return [
            jnp.concatenate([top, dot(w[part:], r, NN)], axis=0) for top, w, r in zip(first, weights, rows, strict=True)
        ]

    def upper_product(weights, rows):
        last = side_by_side([w[part:, part:] for w in weights], [r[part:] for r in rows])
        return [
            jnp.concatenate([dot(w[:part], r, NN), below], axis=0) for below, w, r in zip(last, weights, rows, strict=True)
        ]

    units = [(pair, sub) for pair in pairs for sub in range(rows // SUB)]
    ahead = weights_of(units[0])
    for number, (pair, sub) in enumerate(units):
        grads, grads_t, forward = zip(*ahead, strict=True)
        if number + 1 < len(units):
            ahead = weights_of(units[number + 1])
        span = pl.ds(sub * SUB, SUB)
        places = [head_columns(2 * pair), head_columns(2 * pair + 1)]
        for product, weights, source, out in (
            (lower_product, grads, k, dq),
            (upper_product, grads_t, q, dk),
            (upper_product, forward, o, dv),
        ):
            for at, piece in zip(places, product(weights, [source[span, at] for at in places]), strict=True):
                out[span, at] = piece.astype(PARTIAL)


def part_shapes(rows):
    inner = pltpu.VMEM((GROUP, rows // SUB - 1, HEAD_DIM, HEAD_DIM), jnp.float32)
    return [pltpu.VMEM((rows, GROUP * HEAD_DIM), jnp.bfloat16)] * 4 + [inner] * 2


def states_first_kernel(square, mine, *refs):
    sources, part, sums, sems = refs[:4], refs[-8:-2], refs[-2], refs[-1]
    row = my_row(square)
    for kind in range(2):
        copies = read(square, mine, 0, kind, sources, part[:4], sems)

        @pl.when(row == kind)
        def _():
            start_all(copies)
            sum_kind(kind, copies, part[:4], sums, *part[4:])


def states_first(square, mine, sources, after):
    out = part_shapes(sources[0].shape[0]) + [PIECE]
    *part, sums = pl.pallas_call(
        functools.partial(states_first_kernel, square, mine),
        out_shape=out,
        in_specs=[ANYWHERE] * (4 + len(after)),
        out_specs=[IN_VMEM] * len(out),
        scratch_shapes=[pltpu.SemaphoreType.DMA((4,))],
        compiler_params=pltpu.CompilerParams(vmem_limit_bytes=2 << 20),
        cost_estimate=LONG,
        name="states_first",
    )(*sources, *after)
    return part, sums


def states_second_kernel(square, *refs):
    sources, parts, sums, sems = refs[:4], (refs[-15:-9], refs[-9:-3]), refs[-3:-1], refs[-1]
    copies = {}
    for mine in range(2):
        for kind in range(2):
            copies[mine, kind] = read(square, bool(mine), 1, kind, sources, parts[mine][:4], sems.at[mine])
            start_all(copies[mine, kind])
    for mine in range(2):
        for kind in range(2):
            sum_kind(kind, copies[mine, kind], parts[mine][:4], sums[mine].at[kind], *parts[mine][4:])


def states_second(square, sources, after):
    out = part_shapes(sources[0].shape[0]) * 2 + [state_of(GROUP)] * 2
    result = pl.pallas_call(
        functools.partial(states_second_kernel, square),
        out_shape=out,
        in_specs=[ANYWHERE] * (4 + len(after)),
        out_specs=[IN_VMEM] * len(out),
        scratch_shapes=[pltpu.SemaphoreType.DMA((2, 4))],
        compiler_params=pltpu.CompilerParams(vmem_limit_bytes=2 << 20),
        cost_estimate=LONG,
        name="states_second",
    )(*sources, *after)
    return result[:6], result[6:12], *result[12:]


def states_other_kernel(square, *refs):
    sources, parts, sums, sems = refs[:4], (refs[-15:-9], refs[-9:-3]), refs[-3:-1], refs[-1]
    row = my_row(square)
    copies = {}
    for mine in range(2):
        for kind in range(2):
            copies[mine, kind] = read(square, bool(mine), 0, kind, sources, parts[mine][:4], sems.at[mine])
    for kind in range(2):

        @pl.when(row != kind)
        def _():
            for mine in range(2):
                start_all(copies[mine, kind])
            for mine in range(2):
                sum_kind(kind, copies[mine, kind], parts[mine][:4], sums[mine], *parts[mine][4:])


def states_other(square, sources, other, mine, after):
    out = part_shapes(sources[0].shape[0]) * 2 + [PIECE] * 2
    result = pl.pallas_call(
        functools.partial(states_other_kernel, square),
        out_shape=out,
        in_specs=[ANYWHERE] * 4 + [IN_VMEM] * 12 + [ANYWHERE] * len(after),
        out_specs=[IN_VMEM] * len(out),
        scratch_shapes=[pltpu.SemaphoreType.DMA((2, 4))],
        input_output_aliases={4 + i: i for i in range(12)},
        compiler_params=pltpu.CompilerParams(vmem_limit_bytes=2 << 20),
        cost_estimate=LONG,
        name="states_other",
    )(*sources, *other, *mine, *after)
    return result[:6], result[6:12], *result[12:]


def within_kernel(scale, pairs, *refs):
    work_inside(scale, refs[:4], refs[-3:], pairs)


def within(scale, local, after, pairs=range(GROUP // 2), into=()):
    out = [pltpu.VMEM(local[0].shape, PARTIAL)] * 3
    return pl.pallas_call(
        functools.partial(within_kernel, scale, tuple(pairs)),
        out_shape=out,
        in_specs=[IN_VMEM] * (4 + len(into)) + [ANYWHERE] * len(after),
        out_specs=[IN_VMEM] * 3,
        input_output_aliases={4 + i: i for i in range(len(into))},
        compiler_params=pltpu.CompilerParams(vmem_limit_bytes=3 << 20),
        cost_estimate=LONG,
        name="within",
    )(*local, *into, *after)


def first_group(square, head, start, later):
    upper = my_row(square) == 0
    one, other = start[head], later[head]
    return jnp.where(upper, one, other), jnp.where(upper, other, one)


def second_group(head, rest):
    return rest[0, head], rest[1, head]


def settle(head, prefix, suffix, sums, sums_in, own, other):
    second = my_core() == 1
    own[0, head] = prefix + jnp.where(second, sums_in[0], 0.0)
    own[1, head] = suffix + jnp.where(second, 0.0, sums_in[1])
    other[0, head] = prefix + jnp.where(second, 0.0, sums[0])
    other[1, head] = suffix + jnp.where(second, sums[1], 0.0)


def comes_earlier(turn):
    pair = my_pair()
    return jnp.bitwise_xor(pair, turn) < pair


def sums_of_group(group, head, start, start_in, later, later_in, rest, rest_in):
    if group == 0:
        return first_group(False, head, start, later), first_group(False, head, start_in, later_in)
    return second_group(head, rest), second_group(head, rest_in)


def join_kernel(turns, group, *refs):
    for head in range(GROUP):
        sums, sums_in = sums_of_group(group, head, *refs[:6])
        for turn, out in zip(turns, refs[-len(turns) :], strict=True):
            out[head] = jnp.where(comes_earlier(turn), sums[1] + sums_in[1], sums[0] + sums_in[0])


def combine_kernel(turns, group, *refs):
    received = refs[6 : 6 + len(turns)]
    for head in range(GROUP):
        sums, sums_in = sums_of_group(group, head, *refs[:6])
        prefix = jnp.zeros((HEAD_DIM, HEAD_DIM), jnp.float32)
        suffix = jnp.zeros((HEAD_DIM, HEAD_DIM), jnp.float32)
        for turn, value in zip(turns, received, strict=True):
            earlier = comes_earlier(turn)
            prefix = prefix + jnp.where(earlier, value[head], 0.0)
            suffix = suffix + jnp.where(earlier, 0.0, value[head])
        settle(head, prefix, suffix, sums, sums_in, *refs[-2:])


def row_first_kernel(start, start_in, *refs):
    for head in range(GROUP):
        refs[-1][head] = start[head] + start_in[head]


def row_second_kernel(rest, rest_in, *refs):
    kind = lax.rem(my_pair(), 2)
    for head in range(GROUP):
        refs[-1][head] = rest[kind, head] + rest_in[kind, head]


def column_first_kernel(rest, rest_in, from_row, *refs):
    kind = my_row(True)
    for head in range(GROUP):
        refs[-1][head] = rest[kind, head] + rest_in[kind, head] + from_row[head]


def column_second_kernel(start, start_in, from_row, *refs):
    for head in range(GROUP):
        refs[-1][head] = start[head] + start_in[head] + from_row[head]


def row_third_kernel(later, later_in, from_column, *refs):
    pair = my_pair()
    outer = (pair == 0) | (pair == 3)
    for head in range(GROUP):
        refs[-1][head] = jnp.where(outer, from_column[head], later[head] + later_in[head])


def first_states_kernel(start, start_in, later, later_in, row_second, column_first, *refs):
    pair = my_pair()
    below, right = pair >= 2, lax.rem(pair, 2) == 1
    for head in range(GROUP):
        row, column = row_second[head], column_first[head]
        prefix = jnp.where(right, row, 0.0) + jnp.where(below, column, 0.0)
        suffix = jnp.where(right, 0.0, row) + jnp.where(below, 0.0, column)
        sums, sums_in = first_group(True, head, start, later), first_group(True, head, start_in, later_in)
        settle(head, prefix, suffix, sums, sums_in, *refs[-2:])


def second_states_kernel(rest, rest_in, row_first, row_third, column_second, *refs):
    pair = my_pair()
    below, outer = pair >= 2, (pair == 0) | (pair == 3)
    for head in range(GROUP):
        passed = row_third[head] + jnp.where(outer, column_second[head], 0.0)
        prefix = jnp.where(pair == 1, row_first[head], 0.0) + jnp.where(below, passed, 0.0)
        suffix = jnp.where(pair == 2, row_first[head], 0.0) + jnp.where(below, 0.0, passed)
        settle(head, prefix, suffix, second_group(head, rest), second_group(head, rest_in), *refs[-2:])


def finish_kernel(scale, square, group, halves, *refs):
    targets, staged, sems = refs[-7:-4], refs[-4:-1], refs[-1]
    heads = GROUP
    copies = []
    for number, mine in enumerate(halves):
        k, v, o, dq, dk, dv, state, early, late = refs[9 * number : 9 * number + 9]
        rows = k.shape[0]
        subs = rows // SUB
        base = first_column(square, mine, group)
        for head in range(heads):
            at = head_columns(head)
            to = head_columns(number * heads + head)
            for sub in range(subs):
                span = pl.ds(sub * SUB, SUB)
                before, later = state[0, head], state[1, head]
                if sub > 0:
                    before = before + early[head, sub - 1]
                if sub < subs - 1:
                    later = later + late[head, sub]
                before, later = before.astype(jnp.bfloat16), later.astype(jnp.bfloat16)
                pieces = (
                    dq[span, at] + scale * dot(o[span, at], before, NT),
                    dk[span, at] + scale * dot(v[span, at], later, NT),
                    dv[span, at] + scale * dot(k[span, at], later, NN),
                )
                for out, piece in zip(staged, pieces, strict=True):
                    out[span, to] = piece.astype(jnp.bfloat16)
            if head % 2 == 1 or head == heads - 1:
                first, width = (head - head % 2) * HEAD_DIM, (1 + head % 2) * HEAD_DIM
                for i in range(3):
                    copy = pltpu.make_async_copy(
                        staged[i].at[:, pl.ds(number * heads * HEAD_DIM + first, width)],
                        targets[i].at[:, pl.ds(pl.multiple_of(base + first, HEAD_DIM), width)],
                        sems.at[number, head // 2, i],
                    )
                    copy.start()
                    copies.append(copy)
    for copy in copies:
        copy.wait()


def finish(scale, square, group, parts, before):
    rows = parts[0][1][0].shape[0]
    out = [jax.ShapeDtypeStruct((rows, HEADS * HEAD_DIM), jnp.bfloat16)] * 3
    halves = tuple(part[0] for part in parts)
    operands = []
    for _, local, partials, state, inner in parts:
        operands += [*local[1:], *partials, state, *inner]
    width = len(parts) * GROUP * HEAD_DIM
    return pl.pallas_call(
        functools.partial(finish_kernel, scale, square, group, halves),
        out_shape=out,
        in_specs=[IN_VMEM] * len(operands) + [ANYWHERE] * len(before),
        out_specs=[ANYWHERE] * 3,
        scratch_shapes=[pltpu.VMEM((rows, width), jnp.bfloat16)] * 3
        + [pltpu.SemaphoreType.DMA((len(parts), (GROUP + 1) // 2, 3))],
        input_output_aliases={len(operands) + i: i for i in range(len(before))},
        compiler_params=pltpu.CompilerParams(vmem_limit_bytes=(2 + 3 * len(parts)) << 20),
        cost_estimate=LONG,
        name="finish",
    )(*operands, *before)


def on_device(queries, key_rows, value_rows, out_grad):
    count = lax.axis_size("seq")
    square = count == 8
    scale = (HEAD_DIM * queries.shape[0] * count) ** -0.5
    sources = [
        pltpu.with_memory_space_constraint(array, pltpu.HBM) for array in (queries, key_rows, value_rows, out_grad)
    ]

    def trade(value, distance):
        return lax.ppermute(value, "seq", [(i, i ^ distance) for i in range(count)])

    def run(kernel, out, operands, after):
        return call(kernel, out, operands, after, name=(kernel.func if hasattr(kernel, "func") else kernel).__name__)

    part_eo, start_o = states_first(square, False, sources, ())
    start_in = trade(start_o, 1)
    part_em, start = states_first(square, True, sources, (start_o,))
    after = (start,)
    if square:
        (sent,) = run(row_first_kernel, [PIECE], (start, start_in), ())
        row_first = trade(sent, 2)
        after = (sent,)

    part_lo, part_lm, rest_o, rest = states_second(square, sources, after)
    rest_in = trade(rest_o, 1)
    sums_e, sums_l = (start, start_in), (rest, rest_in)
    partials_lo = within(scale, part_lo[:4], (rest_o,))
    after = (partials_lo[0],)
    if square:
        (sent,) = run(row_second_kernel, [PIECE], sums_l, after)
        row_second = trade(sent, 2)
        partials_lm = within(scale, part_lm[:4], (sent,), range(GROUP // 4))
        (sent,) = run(column_first_kernel, [PIECE], (*sums_l, row_first), (partials_lm[0],))
        column_first = trade(sent, 4)
        after = (sent,)
    else:
        partials_lm = within(scale, part_lm[:4], after, range(GROUP // 4))

    part_eo, part_em, later_o, later = states_other(square, sources, part_eo, part_em, after)
    later_in = trade(later_o, 1)
    sums_b = (later, later_in)
    partials_lm = within(scale, part_lm[:4], (later_o,), range(GROUP // 4, GROUP // 2), partials_lm)
    partials_eo = within(scale, part_eo[:4], (partials_lm[0],))
    if square:
        (sent,) = run(column_second_kernel, [PIECE], (*sums_e, row_second), (partials_eo[0],))
        column_second = trade(sent, 4)
        (sent,) = run(row_third_kernel, [PIECE], (*sums_b, column_first), (sent,))
        row_third = trade(sent, 2)
        arrived = (row_second, column_first)
        own_e, other_e = run(first_states_kernel, STATES, (*sums_e, *sums_b, *arrived), (sent,))
    else:
        turns = range(1, count // 2)
        arrived = []
        sums = (*sums_e, *sums_b, *sums_l)
        for group in range(2):
            kernel = functools.partial(join_kernel, turns, group)
            sent = run(kernel, [PIECE] * len(turns), sums, (partials_eo[0],))
            arrived.append([trade(value, 2 * turn) for turn, value in zip(turns, sent, strict=True)])
        kernel = functools.partial(combine_kernel, turns, 0)
        own_e, other_e = run(kernel, STATES, (*sums, *arrived[0]), ())

    other_e = trade(other_e, 1)
    partials_em = within(scale, part_em[:4], (own_e,))
    parts = [(True, part_em[:4], partials_em, own_e, part_em[4:]), (False, part_eo[:4], partials_eo, other_e, part_eo[4:])]
    done = finish(scale, square, 0, parts, ())

    after = (pltpu.with_memory_space_constraint(done[0], pltpu.HBM),)
    if square:
        arrived = (row_first, row_third, column_second)
        own_l, other_l = run(second_states_kernel, STATES, (*sums_l, *arrived), after)
    else:
        kernel = functools.partial(combine_kernel, turns, 1)
        own_l, other_l = run(kernel, STATES, (*sums, *arrived[1]), after)
    other_l = trade(other_l, 1)
    done = finish(scale, square, 1, [(True, part_lm[:4], partials_lm, own_l, part_lm[4:])], done)
    return tuple(finish(scale, square, 1, [(False, part_lo[:4], partials_lo, other_l, part_lo[4:])], done))


def solution(mesh):
    placed = P(("lists", "seq"), None)
    return jax.shard_map(
        on_device,
        mesh=mesh,
        in_specs=(placed,) * 4,
        out_specs=(placed,) * 3,
        check_vma=False,
    )
```

```python
import functools

import jax
import jax.numpy as jnp
from jax import lax
from jax.experimental import pallas as pl
from jax.experimental.pallas import tpu as pltpu
from jax.sharding import PartitionSpec as P

HEADS = 16
HEAD_DIM = 128
HALF = HEADS // 2
COLUMNS = HALF * HEAD_DIM
GROUP = HALF // 2
SUB = 256
PARTIAL = jnp.float32

TN = (((0,), (0,)), ((), ()))
NT = (((1,), (1,)), ((), ()))
NN = (((1,), (0,)), ((), ()))

IN_VMEM = pl.BlockSpec(memory_space=pltpu.VMEM)
ANYWHERE = pl.BlockSpec(memory_space=pl.ANY)
SHORT = pl.CostEstimate(flops=1000, bytes_accessed=1000, transcendentals=0)
LONG = pl.CostEstimate(flops=2 * 10**10, bytes_accessed=1000, transcendentals=0)


def dot(left, right, dims):
    return lax.dot_general(left, right, dims, preferred_element_type=jnp.float32)


def state_of(heads):
    return pltpu.VMEM((2, heads, HEAD_DIM, HEAD_DIM), jnp.float32)


def head_columns(head):
    return pl.ds(head * HEAD_DIM, HEAD_DIM)


def my_core():
    return lax.rem(lax.axis_index("seq"), 2)


def my_pair():
    return lax.div(lax.axis_index("seq"), 2)


def first_column(square, mine, group):
    half = my_core() if mine else 1 - my_core()
    if square:
        pair = my_pair()
        group = jnp.where((pair == 1) | (pair == 2), 1 - group, group)
    return half * COLUMNS + group * (GROUP * HEAD_DIM)


def my_row(square):
    return lax.div(my_pair(), 2) if square else jnp.int32(0)


PIECE = pltpu.VMEM((GROUP, HEAD_DIM, HEAD_DIM), jnp.float32)
STATES = [state_of(GROUP)] * 2


def call(kernel, out, operands, after=(), scratch=(), cost=SHORT, limit=3, name=None):
    return pl.pallas_call(
        kernel,
        out_shape=out,
        in_specs=[IN_VMEM] * len(operands) + [ANYWHERE] * len(after),
        out_specs=[IN_VMEM] * len(out),
        scratch_shapes=list(scratch),
        compiler_params=pltpu.CompilerParams(vmem_limit_bytes=limit << 20),
        cost_estimate=cost,
        name=name,
    )(*operands, *after)


KINDS = ((1, 2), (0, 3))


def read(square, mine, group, kind, sources, local, sems):
    width = GROUP * HEAD_DIM
    at = pl.ds(pl.multiple_of(first_column(square, mine, group), width), width)
    return [pltpu.make_async_copy(sources[i].at[:, at], local[i], sems.at[i]) for i in KINDS[kind]]


def start_all(copies):
    for copy in copies:
        copy.start()


def sum_kind(kind, copies, local, sums, early, late):
    for copy in copies:
        copy.wait()
    q, k, v, o = local
    left, right = ((k, v), (q, o))[kind]
    subs = q.shape[0] // SUB
    order = list(range(subs)) if kind == 0 else list(range(subs - 1, -1, -1))
    for head in range(GROUP):
        at = head_columns(head)
        total = None
        for sub in order:
            span = pl.ds(sub * SUB, SUB)
            part = dot(left[span, at], right[span, at], TN)
            total = part if total is None else total + part
            if sub != order[-1]:
                if kind == 0:
                    early[head, sub] = total
                else:
                    late[head, sub - 1] = total
        sums[head] = total


def work_inside(scale, local, outs, pairs):
    (q, k, v, o), (dq, dk, dv) = local, outs
    rows = q.shape[0]
    part = SUB // 2
    at_row = lax.broadcasted_iota(jnp.int32, (SUB, SUB), 0)
    at_column = lax.broadcasted_iota(jnp.int32, (SUB, SUB), 1)
    lower = at_row >= at_column
    upper = at_row <= at_column
    nothing = jnp.zeros((part, HEAD_DIM), jnp.bfloat16)

    def weights_of(unit):
        pair, sub = unit
        span = pl.ds(sub * SUB, SUB)
        weights = []
        for head in (2 * pair, 2 * pair + 1):
            at = head_columns(head)
            grads = jnp.where(lower, scale * dot(o[span, at], v[span, at], NT), 0.0).astype(jnp.bfloat16)
            forward = jnp.where(upper, scale * dot(k[span, at], q[span, at], NT), 0.0).astype(jnp.bfloat16)
            weights.append((grads, grads.T, forward))
        return weights

    def side_by_side(weights, rows):
        left = jnp.concatenate([rows[0], nothing], axis=1)
        right = jnp.concatenate([nothing, rows[1]], axis=1)
        product = dot(jnp.concatenate(weights, axis=1), jnp.concatenate([left, right], axis=0), NN)
        return product[:, :HEAD_DIM], product[:, HEAD_DIM:]

    def lower_product(weights, rows):
        first = side_by_side([w[:part, :part] for w in weights], [r[:part] for r in rows])
        return [
            jnp.concatenate([top, dot(w[part:], r, NN)], axis=0) for top, w, r in zip(first, weights, rows, strict=True)
        ]

    def upper_product(weights, rows):
        last = side_by_side([w[part:, part:] for w in weights], [r[part:] for r in rows])
        return [
            jnp.concatenate([dot(w[:part], r, NN), below], axis=0) for below, w, r in zip(last, weights, rows, strict=True)
        ]

    units = [(pair, sub) for pair in pairs for sub in range(rows // SUB)]
    ahead = weights_of(units[0])
    for number, (pair, sub) in enumerate(units):
        grads, grads_t, forward = zip(*ahead, strict=True)
        if number + 1 < len(units):
            ahead = weights_of(units[number + 1])
        span = pl.ds(sub * SUB, SUB)
        places = [head_columns(2 * pair), head_columns(2 * pair + 1)]
        for product, weights, source, out in (
            (lower_product, grads, k, dq),
            (upper_product, grads_t, q, dk),
            (upper_product, forward, o, dv),
        ):
            for at, piece in zip(places, product(weights, [source[span, at] for at in places]), strict=True):
                out[span, at] = piece.astype(PARTIAL)


def part_shapes(rows):
    inner = pltpu.VMEM((GROUP, rows // SUB - 1, HEAD_DIM, HEAD_DIM), jnp.float32)
    return [pltpu.VMEM((rows, GROUP * HEAD_DIM), jnp.bfloat16)] * 4 + [inner] * 2


def states_first_kernel(square, mine, *refs):
    sources, part, sums, sems = refs[:4], refs[-8:-2], refs[-2], refs[-1]
    row = my_row(square)
    for kind in range(2):
        copies = read(square, mine, 0, kind, sources, part[:4], sems)

        @pl.when(row == kind)
        def _():
            start_all(copies)
            sum_kind(kind, copies, part[:4], sums, *part[4:])


def states_first(square, mine, sources, after):
    out = part_shapes(sources[0].shape[0]) + [PIECE]
    *part, sums = pl.pallas_call(
        functools.partial(states_first_kernel, square, mine),
        out_shape=out,
        in_specs=[ANYWHERE] * (4 + len(after)),
        out_specs=[IN_VMEM] * len(out),
        scratch_shapes=[pltpu.SemaphoreType.DMA((4,))],
        compiler_params=pltpu.CompilerParams(vmem_limit_bytes=2 << 20),
        cost_estimate=LONG,
        name="states_first",
    )(*sources, *after)
    return part, sums


def states_second_kernel(square, *refs):
    sources, parts, sums, sems = refs[:4], (refs[-15:-9], refs[-9:-3]), refs[-3:-1], refs[-1]
    copies = {}
    for mine in range(2):
        for kind in range(2):
            copies[mine, kind] = read(square, bool(mine), 1, kind, sources, parts[mine][:4], sems.at[mine])
            start_all(copies[mine, kind])
    for mine in range(2):
        for kind in range(2):
            sum_kind(kind, copies[mine, kind], parts[mine][:4], sums[mine].at[kind], *parts[mine][4:])


def states_second(square, sources, after):
    out = part_shapes(sources[0].shape[0]) * 2 + [state_of(GROUP)] * 2
    result = pl.pallas_call(
        functools.partial(states_second_kernel, square),
        out_shape=out,
        in_specs=[ANYWHERE] * (4 + len(after)),
        out_specs=[IN_VMEM] * len(out),
        scratch_shapes=[pltpu.SemaphoreType.DMA((2, 4))],
        compiler_params=pltpu.CompilerParams(vmem_limit_bytes=2 << 20),
        cost_estimate=LONG,
        name="states_second",
    )(*sources, *after)
    return result[:6], result[6:12], *result[12:]


def states_other_kernel(square, *refs):
    sources, parts, sums, sems = refs[:4], (refs[-15:-9], refs[-9:-3]), refs[-3:-1], refs[-1]
    row = my_row(square)
    copies = {}
    for mine in range(2):
        for kind in range(2):
            copies[mine, kind] = read(square, bool(mine), 0, kind, sources, parts[mine][:4], sems.at[mine])
    for kind in range(2):

        @pl.when(row != kind)
        def _():
            for mine in range(2):
                start_all(copies[mine, kind])
            for mine in range(2):
                sum_kind(kind, copies[mine, kind], parts[mine][:4], sums[mine], *parts[mine][4:])


def states_other(square, sources, other, mine, after):
    out = part_shapes(sources[0].shape[0]) * 2 + [PIECE] * 2
    result = pl.pallas_call(
        functools.partial(states_other_kernel, square),
        out_shape=out,
        in_specs=[ANYWHERE] * 4 + [IN_VMEM] * 12 + [ANYWHERE] * len(after),
        out_specs=[IN_VMEM] * len(out),
        scratch_shapes=[pltpu.SemaphoreType.DMA((2, 4))],
        input_output_aliases={4 + i: i for i in range(12)},
        compiler_params=pltpu.CompilerParams(vmem_limit_bytes=2 << 20),
        cost_estimate=LONG,
        name="states_other",
    )(*sources, *other, *mine, *after)
    return result[:6], result[6:12], *result[12:]


def within_kernel(scale, pairs, *refs):
    work_inside(scale, refs[:4], refs[-3:], pairs)


def within(scale, local, after, pairs=range(GROUP // 2), into=()):
    out = [pltpu.VMEM(local[0].shape, PARTIAL)] * 3
    return pl.pallas_call(
        functools.partial(within_kernel, scale, tuple(pairs)),
        out_shape=out,
        in_specs=[IN_VMEM] * (4 + len(into)) + [ANYWHERE] * len(after),
        out_specs=[IN_VMEM] * 3,
        input_output_aliases={4 + i: i for i in range(len(into))},
        compiler_params=pltpu.CompilerParams(vmem_limit_bytes=3 << 20),
        cost_estimate=LONG,
        name="within",
    )(*local, *into, *after)


def first_group(square, head, start, later):
    upper = my_row(square) == 0
    one, other = start[head], later[head]
    return jnp.where(upper, one, other), jnp.where(upper, other, one)


def second_group(head, rest):
    return rest[0, head], rest[1, head]


def settle(head, prefix, suffix, sums, sums_in, own, other):
    second = my_core() == 1
    own[0, head] = prefix + jnp.where(second, sums_in[0], 0.0)
    own[1, head] = suffix + jnp.where(second, 0.0, sums_in[1])
    other[0, head] = prefix + jnp.where(second, 0.0, sums[0])
    other[1, head] = suffix + jnp.where(second, sums[1], 0.0)


def comes_earlier(turn):
    pair = my_pair()
    return jnp.bitwise_xor(pair, turn) < pair


def sums_of_group(group, head, start, start_in, later, later_in, rest, rest_in):
    if group == 0:
        return first_group(False, head, start, later), first_group(False, head, start_in, later_in)
    return second_group(head, rest), second_group(head, rest_in)


def join_kernel(turns, group, *refs):
    for head in range(GROUP):
        sums, sums_in = sums_of_group(group, head, *refs[:6])
        for turn, out in zip(turns, refs[-len(turns) :], strict=True):
            out[head] = jnp.where(comes_earlier(turn), sums[1] + sums_in[1], sums[0] + sums_in[0])


def combine_kernel(turns, group, *refs):
    received = refs[6 : 6 + len(turns)]
    for head in range(GROUP):
        sums, sums_in = sums_of_group(group, head, *refs[:6])
        prefix = jnp.zeros((HEAD_DIM, HEAD_DIM), jnp.float32)
        suffix = jnp.zeros((HEAD_DIM, HEAD_DIM), jnp.float32)
        for turn, value in zip(turns, received, strict=True):
            earlier = comes_earlier(turn)
            prefix = prefix + jnp.where(earlier, value[head], 0.0)
            suffix = suffix + jnp.where(earlier, 0.0, value[head])
        settle(head, prefix, suffix, sums, sums_in, *refs[-2:])


def row_first_kernel(start, start_in, *refs):
    for head in range(GROUP):
        refs[-1][head] = start[head] + start_in[head]


def row_second_kernel(rest, rest_in, *refs):
    kind = lax.rem(my_pair(), 2)
    for head in range(GROUP):
        refs[-1][head] = rest[kind, head] + rest_in[kind, head]


def column_first_kernel(rest, rest_in, from_row, *refs):
    kind = my_row(True)
    for head in range(GROUP):
        refs[-1][head] = rest[kind, head] + rest_in[kind, head] + from_row[head]


def column_second_kernel(start, start_in, from_row, *refs):
    for head in range(GROUP):
        refs[-1][head] = start[head] + start_in[head] + from_row[head]


def row_third_kernel(later, later_in, from_column, *refs):
    pair = my_pair()
    outer = (pair == 0) | (pair == 3)
    for head in range(GROUP):
        refs[-1][head] = jnp.where(outer, from_column[head], later[head] + later_in[head])


def first_states_kernel(start, start_in, later, later_in, rest, rest_in, row_first, row_second, column_first, *refs):
    own, other, own_prefix = refs[-3:]
    second = my_core() == 1
    pair = my_pair()
    below, right = pair >= 2, lax.rem(pair, 2) == 1
    for head in range(GROUP):
        row, column = row_second[head], column_first[head]
        prefix = jnp.where(right, row, 0.0) + jnp.where(below, column, 0.0)
        suffix = jnp.where(right, 0.0, row) + jnp.where(below, 0.0, column)
        sums, sums_in = first_group(True, head, start, later), first_group(True, head, start_in, later_in)
        settle(head, prefix, suffix, sums, sums_in, own, other.at[pl.ds(0, 2)])
        prefix = jnp.where(pair == 1, row_first[head], 0.0)
        own_prefix[head] = prefix + jnp.where(second, rest_in[0, head], 0.0)
        other[2, head] = prefix + jnp.where(second, 0.0, rest[0, head])


def second_states_kernel(rest, rest_in, row_first, row_third, column_second, *refs):
    pair = my_pair()
    below, outer = pair >= 2, (pair == 0) | (pair == 3)
    for head in range(GROUP):
        passed = row_third[head] + jnp.where(outer, column_second[head], 0.0)
        prefix = jnp.where(pair == 1, row_first[head], 0.0) + jnp.where(below, passed, 0.0)
        suffix = jnp.where(pair == 2, row_first[head], 0.0) + jnp.where(below, 0.0, passed)
        settle(head, prefix, suffix, second_group(head, rest), second_group(head, rest_in), *refs[-2:])


def add_state(scale, head, partial, rows, states, inner, dims, out, to):
    at = head_columns(head)
    subs = rows.shape[0] // SUB
    for sub in range(subs):
        span = pl.ds(sub * SUB, SUB)
        state = states[head]
        if dims[1] == 0:
            state = state + inner[head, sub - 1] if sub > 0 else state
        else:
            state = state + inner[head, sub] if sub < subs - 1 else state
        piece = partial[span, at] + scale * dot(rows[span, at], state.astype(jnp.bfloat16), dims[0])
        out[span, to] = piece.astype(jnp.bfloat16)


QUERY, KEY, VALUE = (NT, 0), (NT, 1), (NN, 1)


def finish_kernel(scale, square, group, halves, ahead, *refs):
    targets, staged, sems = refs[-7:-4], refs[-4:-1], refs[-1]
    row = my_row(square)

    def copies_of(i, number, which, first, heads):
        mine, at_group = halves[number % len(halves)], 1 if number >= len(halves) else group
        width = heads * HEAD_DIM
        column = first_column(square, mine, at_group) + first * HEAD_DIM
        return pltpu.make_async_copy(
            staged[i].at[:, pl.ds((number * GROUP + first) * HEAD_DIM, width)],
            targets[i].at[:, pl.ds(pl.multiple_of(column, HEAD_DIM), width)],
            sems.at[number, which, i],
        )

    def run(i, number, copies, partial, rows, states, inner, dims):
        for head in range(GROUP):
            to = head_columns(number * GROUP + head)
            add_state(scale, head, partial, rows, states, inner, dims, staged[i], to)
            if head % 2 == 1:
                copies[head // 2].start()

    def pieces(i, number):
        return [copies_of(i, number, which, 2 * which, 2) for which in range(GROUP // 2)]

    sometimes, always = [], []
    for number in range(len(halves)):
        k, v, o, dq, dk, dv, state, early, late = refs[9 * number : 9 * number + 9]
        query = pieces(0, number)
        if square and group == 1:
            sometimes += query

            @pl.when(row == 1)
            def _():
                run(0, number, query, dq, o, state.at[0], early, QUERY)
        else:
            always += query
            run(0, number, query, dq, o, state.at[0], early, QUERY)
        for i, arguments in ((1, (dk, v, state.at[1], late, KEY)), (2, (dv, k, state.at[1], late, VALUE))):
            copies = pieces(i, number)
            always += copies
            run(i, number, copies, *arguments)
    rest = refs[9 * len(halves) :]
    for n in range(ahead):
        number = len(halves) + n
        o, dq, prefix, early = rest[4 * n : 4 * n + 4]
        prefix = prefix if n == 0 else prefix.at[2]
        query = pieces(0, number)
        sometimes += query

        @pl.when(row == 0)
        def _():
            run(0, number, query, dq, o, prefix, early, QUERY)

    for copy in always:
        copy.wait()
    if sometimes:

        @pl.when(row == (0 if ahead else 1))
        def _():
            for copy in sometimes:
                copy.wait()


def finish(scale, square, group, parts, before, ahead=()):
    rows = parts[0][1][0].shape[0]
    out = [jax.ShapeDtypeStruct((rows, HEADS * HEAD_DIM), jnp.bfloat16)] * 3
    halves = tuple(part[0] for part in parts)
    operands = []
    for _, local, partials, state, inner in parts:
        operands += [*local[1:], *partials, state, *inner]
    for arrays in ahead:
        operands += arrays
    widths = [(len(parts) + extra) * GROUP * HEAD_DIM for extra in (len(ahead), 0, 0)]
    return pl.pallas_call(
        functools.partial(finish_kernel, scale, square, group, halves, len(ahead)),
        out_shape=out,
        in_specs=[IN_VMEM] * len(operands) + [ANYWHERE] * len(before),
        out_specs=[ANYWHERE] * 3,
        scratch_shapes=[pltpu.VMEM((rows, width), jnp.bfloat16) for width in widths]
        + [pltpu.SemaphoreType.DMA((len(parts) + len(ahead), GROUP // 2, 3))],
        input_output_aliases={len(operands) + i: i for i in range(len(before))},
        compiler_params=pltpu.CompilerParams(vmem_limit_bytes=(2 + 3 * len(parts) + len(ahead)) << 20),
        cost_estimate=LONG,
        name="finish",
    )(*operands, *before)


def on_device(queries, key_rows, value_rows, out_grad):
    count = lax.axis_size("seq")
    square = count == 8
    scale = (HEAD_DIM * queries.shape[0] * count) ** -0.5
    sources = [
        pltpu.with_memory_space_constraint(array, pltpu.HBM) for array in (queries, key_rows, value_rows, out_grad)
    ]

    def trade(value, distance):
        return lax.ppermute(value, "seq", [(i, i ^ distance) for i in range(count)])

    def run(kernel, out, operands, after):
        return call(kernel, out, operands, after, name=(kernel.func if hasattr(kernel, "func") else kernel).__name__)

    part_eo, start_o = states_first(square, False, sources, ())
    start_in = trade(start_o, 1)
    part_em, start = states_first(square, True, sources, (start_o,))
    after = (start,)
    if square:
        (sent,) = run(row_first_kernel, [PIECE], (start, start_in), ())
        row_first = trade(sent, 2)
        after = (sent,)

    part_lo, part_lm, rest_o, rest = states_second(square, sources, after)
    rest_in = trade(rest_o, 1)
    sums_e, sums_l = (start, start_in), (rest, rest_in)
    partials_lo = within(scale, part_lo[:4], (rest_o,))
    after = (partials_lo[0],)
    if square:
        (sent,) = run(row_second_kernel, [PIECE], sums_l, after)
        row_second = trade(sent, 2)
        partials_lm = within(scale, part_lm[:4], (sent,), range(GROUP // 4))
        (sent,) = run(column_first_kernel, [PIECE], (*sums_l, row_first), (partials_lm[0],))
        column_first = trade(sent, 4)
        after = (sent,)
    else:
        partials_lm = within(scale, part_lm[:4], after, range(GROUP // 4))

    part_eo, part_em, later_o, later = states_other(square, sources, part_eo, part_em, after)
    later_in = trade(later_o, 1)
    sums_b = (later, later_in)
    partials_lm = within(scale, part_lm[:4], (later_o,), range(GROUP // 4, GROUP // 2), partials_lm)
    partials_eo = within(scale, part_eo[:4], (partials_lm[0],))
    if square:
        (sent,) = run(column_second_kernel, [PIECE], (*sums_e, row_second), (partials_eo[0],))
        column_second = trade(sent, 4)
        (sent,) = run(row_third_kernel, [PIECE], (*sums_b, column_first), (sent,))
        row_third = trade(sent, 2)
        arrived = (row_first, row_second, column_first)
        out = [state_of(GROUP), pltpu.VMEM((3, GROUP, HEAD_DIM, HEAD_DIM), jnp.float32), PIECE]
        own_e, other_e, own_prefix = run(first_states_kernel, out, (*sums_e, *sums_b, *sums_l, *arrived), (sent,))
    else:
        turns = range(1, count // 2)
        arrived = []
        sums = (*sums_e, *sums_b, *sums_l)
        for group in range(2):
            kernel = functools.partial(join_kernel, turns, group)
            sent = run(kernel, [PIECE] * len(turns), sums, (partials_eo[0],))
            arrived.append([trade(value, 2 * turn) for turn, value in zip(turns, sent, strict=True)])
        kernel = functools.partial(combine_kernel, turns, 0)
        own_e, other_e = run(kernel, STATES, (*sums, *arrived[0]), ())

    other_e = trade(other_e, 1)
    partials_em = within(scale, part_em[:4], (own_e,))
    parts = [(True, part_em[:4], partials_em, own_e, part_em[4:]), (False, part_eo[:4], partials_eo, other_e, part_eo[4:])]
    ahead = ()
    if square:
        ahead = (
            (part_lm[3], partials_lm[0], own_prefix, part_lm[4]),
            (part_lo[3], partials_lo[0], other_e, part_lo[4]),
        )
    done = finish(scale, square, 0, parts, (), ahead)

    after = (pltpu.with_memory_space_constraint(done[0], pltpu.HBM),)
    if square:
        arrived = (row_first, row_third, column_second)
        own_l, other_l = run(second_states_kernel, STATES, (*sums_l, *arrived), after)
    else:
        kernel = functools.partial(combine_kernel, turns, 1)
        own_l, other_l = run(kernel, STATES, (*sums, *arrived[1]), after)
    other_l = trade(other_l, 1)
    done = finish(scale, square, 1, [(True, part_lm[:4], partials_lm, own_l, part_lm[4:])], done)
    return tuple(finish(scale, square, 1, [(False, part_lo[:4], partials_lo, other_l, part_lo[4:])], done))


def solution(mesh):
    placed = P(("lists", "seq"), None)
    return jax.shard_map(
        on_device,
        mesh=mesh,
        in_specs=(placed,) * 4,
        out_specs=(placed,) * 3,
        check_vma=False,
    )
```

```python
import functools

import jax
import jax.numpy as jnp
from jax import lax
from jax.experimental import pallas as pl
from jax.experimental.pallas import tpu as pltpu
from jax.sharding import PartitionSpec as P

HEADS = 16
HEAD_DIM = 128
HALF = HEADS // 2
COLUMNS = HALF * HEAD_DIM
GROUP = HALF // 2
SUB = 256
PARTIAL = jnp.float32

TN = (((0,), (0,)), ((), ()))
NT = (((1,), (1,)), ((), ()))
NN = (((1,), (0,)), ((), ()))

IN_VMEM = pl.BlockSpec(memory_space=pltpu.VMEM)
ANYWHERE = pl.BlockSpec(memory_space=pl.ANY)
SHORT = pl.CostEstimate(flops=1000, bytes_accessed=1000, transcendentals=0)
LONG = pl.CostEstimate(flops=2 * 10**10, bytes_accessed=1000, transcendentals=0)


def dot(left, right, dims):
    return lax.dot_general(left, right, dims, preferred_element_type=jnp.float32)


def state_of(heads):
    return pltpu.VMEM((2, heads, HEAD_DIM, HEAD_DIM), jnp.float32)


def head_columns(head):
    return pl.ds(head * HEAD_DIM, HEAD_DIM)


def my_core():
    return lax.rem(lax.axis_index("seq"), 2)


def my_pair():
    return lax.div(lax.axis_index("seq"), 2)


def first_column(square, mine, group):
    half = my_core() if mine else 1 - my_core()
    if square:
        pair = my_pair()
        group = jnp.where((pair == 1) | (pair == 2), 1 - group, group)
    return half * COLUMNS + group * (GROUP * HEAD_DIM)


def my_row(square):
    return lax.div(my_pair(), 2) if square else jnp.int32(0)


PIECE = pltpu.VMEM((GROUP, HEAD_DIM, HEAD_DIM), jnp.float32)
STATES = [state_of(GROUP)] * 2


def call(kernel, out, operands, after=(), scratch=(), cost=SHORT, limit=3, name=None):
    return pl.pallas_call(
        kernel,
        out_shape=out,
        in_specs=[IN_VMEM] * len(operands) + [ANYWHERE] * len(after),
        out_specs=[IN_VMEM] * len(out),
        scratch_shapes=list(scratch),
        compiler_params=pltpu.CompilerParams(vmem_limit_bytes=limit << 20),
        cost_estimate=cost,
        name=name,
    )(*operands, *after)


KINDS = ((1, 2), (0, 3))


def read(square, mine, group, kind, sources, local, sems):
    width = GROUP * HEAD_DIM
    at = pl.ds(pl.multiple_of(first_column(square, mine, group), width), width)
    return [pltpu.make_async_copy(sources[i].at[:, at], local[i], sems.at[i]) for i in KINDS[kind]]


def start_all(copies):
    for copy in copies:
        copy.start()


def sum_kind(kind, copies, local, sums, early, late):
    for copy in copies:
        copy.wait()
    q, k, v, o = local
    left, right = ((k, v), (q, o))[kind]
    subs = q.shape[0] // SUB
    order = list(range(subs)) if kind == 0 else list(range(subs - 1, -1, -1))
    for head in range(GROUP):
        at = head_columns(head)
        total = None
        for sub in order:
            span = pl.ds(sub * SUB, SUB)
            part = dot(left[span, at], right[span, at], TN)
            total = part if total is None else total + part
            if sub != order[-1]:
                if kind == 0:
                    early[head, sub] = total
                else:
                    late[head, sub - 1] = total
        sums[head] = total


def work_inside(scale, local, outs, pairs):
    (q, k, v, o), (dq, dk, dv) = local, outs
    rows = q.shape[0]
    part = SUB // 2
    at_row = lax.broadcasted_iota(jnp.int32, (SUB, SUB), 0)
    at_column = lax.broadcasted_iota(jnp.int32, (SUB, SUB), 1)
    lower = at_row >= at_column
    upper = at_row <= at_column
    nothing = jnp.zeros((part, HEAD_DIM), jnp.bfloat16)

    def weights_of(unit):
        pair, sub = unit
        span = pl.ds(sub * SUB, SUB)
        weights = []
        for head in (2 * pair, 2 * pair + 1):
            at = head_columns(head)
            grads = jnp.where(lower, scale * dot(o[span, at], v[span, at], NT), 0.0).astype(jnp.bfloat16)
            forward = jnp.where(upper, scale * dot(k[span, at], q[span, at], NT), 0.0).astype(jnp.bfloat16)
            weights.append((grads, grads.T, forward))
        return weights

    def side_by_side(weights, rows):
        left = jnp.concatenate([rows[0], nothing], axis=1)
        right = jnp.concatenate([nothing, rows[1]], axis=1)
        product = dot(jnp.concatenate(weights, axis=1), jnp.concatenate([left, right], axis=0), NN)
        return product[:, :HEAD_DIM], product[:, HEAD_DIM:]

    def lower_product(weights, rows):
        first = side_by_side([w[:part, :part] for w in weights], [r[:part] for r in rows])
        return [
            jnp.concatenate([top, dot(w[part:], r, NN)], axis=0) for top, w, r in zip(first, weights, rows, strict=True)
        ]

    def upper_product(weights, rows):
        last = side_by_side([w[part:, part:] for w in weights], [r[part:] for r in rows])
        return [
            jnp.concatenate([dot(w[:part], r, NN), below], axis=0) for below, w, r in zip(last, weights, rows, strict=True)
        ]

    units = [(pair, sub) for pair in pairs for sub in range(rows // SUB)]
    ahead = weights_of(units[0])
    for number, (pair, sub) in enumerate(units):
        grads, grads_t, forward = zip(*ahead, strict=True)
        if number + 1 < len(units):
            ahead = weights_of(units[number + 1])
        span = pl.ds(sub * SUB, SUB)
        places = [head_columns(2 * pair), head_columns(2 * pair + 1)]
        for product, weights, source, out in (
            (lower_product, grads, k, dq),
            (upper_product, grads_t, q, dk),
            (upper_product, forward, o, dv),
        ):
            for at, piece in zip(places, product(weights, [source[span, at] for at in places]), strict=True):
                out[span, at] = piece.astype(PARTIAL)


def part_shapes(rows):
    inner = pltpu.VMEM((GROUP, rows // SUB - 1, HEAD_DIM, HEAD_DIM), jnp.float32)
    return [pltpu.VMEM((rows, GROUP * HEAD_DIM), jnp.bfloat16)] * 4 + [inner] * 2


def states_first_kernel(square, *refs):
    sources, part, local, sums, sems = refs[:4], refs[4:10], refs[10:14], refs[14], refs[15]
    row = my_row(square)
    for kind in range(2):
        copies = read(square, False, 0, kind, sources, part[:4], sems.at[0])
        behind = read(square, True, 0, kind, sources, local, sems.at[1])

        @pl.when(row == kind)
        def _():
            start_all(copies)
            start_all(behind)
            sum_kind(kind, copies, part[:4], sums, *part[4:])
            for copy in behind:
                copy.wait()


def states_first(square, sources):
    part = part_shapes(sources[0].shape[0])
    out = part + part[:4] + [PIECE]
    result = pl.pallas_call(
        functools.partial(states_first_kernel, square),
        out_shape=out,
        in_specs=[ANYWHERE] * 4,
        out_specs=[IN_VMEM] * len(out),
        scratch_shapes=[pltpu.SemaphoreType.DMA((2, 4))],
        compiler_params=pltpu.CompilerParams(vmem_limit_bytes=2 << 20),
        cost_estimate=LONG,
        name="states_first",
    )(*sources)
    return result[:6], result[6:10], result[10]


def states_mine_kernel(square, *refs):
    local, inner, sums = refs[:4], refs[-3:-1], refs[-1]
    row = my_row(square)
    for kind in range(2):

        @pl.when(row == kind)
        def _():
            sum_kind(kind, (), local, sums, *inner)


def states_mine(square, local, after):
    inner = part_shapes(local[0].shape[0])[4:]
    out = [*inner, PIECE]
    kernel = functools.partial(states_mine_kernel, square)
    *inner, sums = call(kernel, out, local, after, cost=LONG, limit=2, name="states_mine")
    return [*local, *inner], sums


def states_second_kernel(square, *refs):
    sources, parts, sums, sems = refs[:4], (refs[-15:-9], refs[-9:-3]), refs[-3:-1], refs[-1]
    copies = {}
    for mine in range(2):
        for kind in range(2):
            copies[mine, kind] = read(square, bool(mine), 1, kind, sources, parts[mine][:4], sems.at[mine])
            start_all(copies[mine, kind])
    for mine in range(2):
        for kind in range(2):
            sum_kind(kind, copies[mine, kind], parts[mine][:4], sums[mine].at[kind], *parts[mine][4:])


def states_second(square, sources, after):
    out = part_shapes(sources[0].shape[0]) * 2 + [state_of(GROUP)] * 2
    result = pl.pallas_call(
        functools.partial(states_second_kernel, square),
        out_shape=out,
        in_specs=[ANYWHERE] * (4 + len(after)),
        out_specs=[IN_VMEM] * len(out),
        scratch_shapes=[pltpu.SemaphoreType.DMA((2, 4))],
        compiler_params=pltpu.CompilerParams(vmem_limit_bytes=2 << 20),
        cost_estimate=LONG,
        name="states_second",
    )(*sources, *after)
    return result[:6], result[6:12], *result[12:]


def states_other_kernel(square, *refs):
    sources, parts, sums, sems = refs[:4], (refs[-15:-9], refs[-9:-3]), refs[-3:-1], refs[-1]
    row = my_row(square)
    copies = {}
    for mine in range(2):
        for kind in range(2):
            copies[mine, kind] = read(square, bool(mine), 0, kind, sources, parts[mine][:4], sems.at[mine])
    for kind in range(2):

        @pl.when(row != kind)
        def _():
            for mine in range(2):
                start_all(copies[mine, kind])
            for mine in range(2):
                sum_kind(kind, copies[mine, kind], parts[mine][:4], sums[mine], *parts[mine][4:])


def states_other(square, sources, other, mine, after):
    out = part_shapes(sources[0].shape[0]) * 2 + [PIECE] * 2
    result = pl.pallas_call(
        functools.partial(states_other_kernel, square),
        out_shape=out,
        in_specs=[ANYWHERE] * 4 + [IN_VMEM] * 12 + [ANYWHERE] * len(after),
        out_specs=[IN_VMEM] * len(out),
        scratch_shapes=[pltpu.SemaphoreType.DMA((2, 4))],
        input_output_aliases={4 + i: i for i in range(12)},
        compiler_params=pltpu.CompilerParams(vmem_limit_bytes=2 << 20),
        cost_estimate=LONG,
        name="states_other",
    )(*sources, *other, *mine, *after)
    return result[:6], result[6:12], *result[12:]


def within_kernel(scale, pairs, *refs):
    work_inside(scale, refs[:4], refs[-3:], pairs)


def within(scale, local, after, pairs=range(GROUP // 2), into=()):
    out = [pltpu.VMEM(local[0].shape, PARTIAL)] * 3
    return pl.pallas_call(
        functools.partial(within_kernel, scale, tuple(pairs)),
        out_shape=out,
        in_specs=[IN_VMEM] * (4 + len(into)) + [ANYWHERE] * len(after),
        out_specs=[IN_VMEM] * 3,
        input_output_aliases={4 + i: i for i in range(len(into))},
        compiler_params=pltpu.CompilerParams(vmem_limit_bytes=3 << 20),
        cost_estimate=LONG,
        name="within",
    )(*local, *into, *after)


def first_group(square, head, start, later):
    upper = my_row(square) == 0
    one, other = start[head], later[head]
    return jnp.where(upper, one, other), jnp.where(upper, other, one)


def second_group(head, rest):
    return rest[0, head], rest[1, head]


def settle(head, prefix, suffix, sums, sums_in, own, other):
    second = my_core() == 1
    own[0, head] = prefix + jnp.where(second, sums_in[0], 0.0)
    own[1, head] = suffix + jnp.where(second, 0.0, sums_in[1])
    other[0, head] = prefix + jnp.where(second, 0.0, sums[0])
    other[1, head] = suffix + jnp.where(second, sums[1], 0.0)


def comes_earlier(turn):
    pair = my_pair()
    return jnp.bitwise_xor(pair, turn) < pair


def sums_of_group(group, head, start, start_in, later, later_in, rest, rest_in):
    if group == 0:
        return first_group(False, head, start, later), first_group(False, head, start_in, later_in)
    return second_group(head, rest), second_group(head, rest_in)


def join_kernel(turns, group, *refs):
    for head in range(GROUP):
        sums, sums_in = sums_of_group(group, head, *refs[:6])
        for turn, out in zip(turns, refs[-len(turns) :], strict=True):
            out[head] = jnp.where(comes_earlier(turn), sums[1] + sums_in[1], sums[0] + sums_in[0])


def combine_kernel(turns, group, *refs):
    received = refs[6 : 6 + len(turns)]
    for head in range(GROUP):
        sums, sums_in = sums_of_group(group, head, *refs[:6])
        prefix = jnp.zeros((HEAD_DIM, HEAD_DIM), jnp.float32)
        suffix = jnp.zeros((HEAD_DIM, HEAD_DIM), jnp.float32)
        for turn, value in zip(turns, received, strict=True):
            earlier = comes_earlier(turn)
            prefix = prefix + jnp.where(earlier, value[head], 0.0)
            suffix = suffix + jnp.where(earlier, 0.0, value[head])
        settle(head, prefix, suffix, sums, sums_in, *refs[-2:])


def row_first_kernel(start, start_in, *refs):
    for head in range(GROUP):
        refs[-1][head] = start[head] + start_in[head]


def row_second_kernel(rest, rest_in, *refs):
    kind = lax.rem(my_pair(), 2)
    for head in range(GROUP):
        refs[-1][head] = rest[kind, head] + rest_in[kind, head]


def column_first_kernel(rest, rest_in, from_row, *refs):
    kind = my_row(True)
    for head in range(GROUP):
        refs[-1][head] = rest[kind, head] + rest_in[kind, head] + from_row[head]


def column_second_kernel(start, start_in, from_row, *refs):
    for head in range(GROUP):
        refs[-1][head] = start[head] + start_in[head] + from_row[head]


def row_third_kernel(later, later_in, from_column, *refs):
    pair = my_pair()
    outer = (pair == 0) | (pair == 3)
    for head in range(GROUP):
        refs[-1][head] = jnp.where(outer, from_column[head], later[head] + later_in[head])


def first_states_kernel(start, start_in, later, later_in, rest, rest_in, row_first, row_second, column_first, *refs):
    own, other, own_prefix = refs[-3:]
    second = my_core() == 1
    pair = my_pair()
    below, right = pair >= 2, lax.rem(pair, 2) == 1
    for head in range(GROUP):
        row, column = row_second[head], column_first[head]
        prefix = jnp.where(right, row, 0.0) + jnp.where(below, column, 0.0)
        suffix = jnp.where(right, 0.0, row) + jnp.where(below, 0.0, column)
        sums, sums_in = first_group(True, head, start, later), first_group(True, head, start_in, later_in)
        settle(head, prefix, suffix, sums, sums_in, own, other.at[pl.ds(0, 2)])
        prefix = jnp.where(pair == 1, row_first[head], 0.0)
        own_prefix[head] = prefix + jnp.where(second, rest_in[0, head], 0.0)
        other[2, head] = prefix + jnp.where(second, 0.0, rest[0, head])


def second_states_kernel(rest, rest_in, row_first, row_third, column_second, *refs):
    pair = my_pair()
    below, outer = pair >= 2, (pair == 0) | (pair == 3)
    for head in range(GROUP):
        passed = row_third[head] + jnp.where(outer, column_second[head], 0.0)
        prefix = jnp.where(pair == 1, row_first[head], 0.0) + jnp.where(below, passed, 0.0)
        suffix = jnp.where(pair == 2, row_first[head], 0.0) + jnp.where(below, 0.0, passed)
        settle(head, prefix, suffix, second_group(head, rest), second_group(head, rest_in), *refs[-2:])


def add_state(scale, head, partial, rows, states, inner, dims, out, to):
    at = head_columns(head)
    subs = rows.shape[0] // SUB
    for sub in range(subs):
        span = pl.ds(sub * SUB, SUB)
        state = states[head]
        if dims[1] == 0:
            state = state + inner[head, sub - 1] if sub > 0 else state
        else:
            state = state + inner[head, sub] if sub < subs - 1 else state
        piece = partial[span, at] + scale * dot(rows[span, at], state.astype(jnp.bfloat16), dims[0])
        out[span, to] = piece.astype(jnp.bfloat16)


QUERY, KEY, VALUE = (NT, 0), (NT, 1), (NN, 1)


def finish_kernel(scale, square, group, halves, ahead, *refs):
    targets, staged, sems = refs[-7:-4], refs[-4:-1], refs[-1]
    row = my_row(square)

    def copies_of(i, number, which, first, heads):
        mine, at_group = halves[number % len(halves)], 1 if number >= len(halves) else group
        width = heads * HEAD_DIM
        column = first_column(square, mine, at_group) + first * HEAD_DIM
        return pltpu.make_async_copy(
            staged[i].at[:, pl.ds((number * GROUP + first) * HEAD_DIM, width)],
            targets[i].at[:, pl.ds(pl.multiple_of(column, HEAD_DIM), width)],
            sems.at[number, which, i],
        )

    def run(i, number, copies, partial, rows, states, inner, dims):
        for head in range(GROUP):
            to = head_columns(number * GROUP + head)
            add_state(scale, head, partial, rows, states, inner, dims, staged[i], to)
            if head % 2 == 1:
                copies[head // 2].start()

    def pieces(i, number):
        return [copies_of(i, number, which, 2 * which, 2) for which in range(GROUP // 2)]

    sometimes, always = [], []
    for number in range(len(halves)):
        k, v, o, dq, dk, dv, state, early, late = refs[9 * number : 9 * number + 9]
        query = pieces(0, number)
        if square and group == 1:
            sometimes += query

            @pl.when(row == 1)
            def _():
                run(0, number, query, dq, o, state.at[0], early, QUERY)
        else:
            always += query
            run(0, number, query, dq, o, state.at[0], early, QUERY)
        for i, arguments in ((1, (dk, v, state.at[1], late, KEY)), (2, (dv, k, state.at[1], late, VALUE))):
            copies = pieces(i, number)
            always += copies
            run(i, number, copies, *arguments)
    rest = refs[9 * len(halves) :]
    for n in range(ahead):
        number = len(halves) + n
        o, dq, prefix, early = rest[4 * n : 4 * n + 4]
        prefix = prefix if n == 0 else prefix.at[2]
        query = pieces(0, number)
        sometimes += query

        @pl.when(row == 0)
        def _():
            run(0, number, query, dq, o, prefix, early, QUERY)

    for copy in always:
        copy.wait()
    if sometimes:

        @pl.when(row == (0 if ahead else 1))
        def _():
            for copy in sometimes:
                copy.wait()


def finish(scale, square, group, parts, before, ahead=()):
    rows = parts[0][1][0].shape[0]
    out = [jax.ShapeDtypeStruct((rows, HEADS * HEAD_DIM), jnp.bfloat16)] * 3
    halves = tuple(part[0] for part in parts)
    operands = []
    for _, local, partials, state, inner in parts:
        operands += [*local[1:], *partials, state, *inner]
    for arrays in ahead:
        operands += arrays
    widths = [(len(parts) + extra) * GROUP * HEAD_DIM for extra in (len(ahead), 0, 0)]
    return pl.pallas_call(
        functools.partial(finish_kernel, scale, square, group, halves, len(ahead)),
        out_shape=out,
        in_specs=[IN_VMEM] * len(operands) + [ANYWHERE] * len(before),
        out_specs=[ANYWHERE] * 3,
        scratch_shapes=[pltpu.VMEM((rows, width), jnp.bfloat16) for width in widths]
        + [pltpu.SemaphoreType.DMA((len(parts) + len(ahead), GROUP // 2, 3))],
        input_output_aliases={len(operands) + i: i for i in range(len(before))},
        compiler_params=pltpu.CompilerParams(vmem_limit_bytes=(2 + 3 * len(parts) + len(ahead)) << 20),
        cost_estimate=LONG,
        name="finish",
    )(*operands, *before)


def on_device(queries, key_rows, value_rows, out_grad):
    count = lax.axis_size("seq")
    square = count == 8
    scale = (HEAD_DIM * queries.shape[0] * count) ** -0.5
    sources = [
        pltpu.with_memory_space_constraint(array, pltpu.HBM) for array in (queries, key_rows, value_rows, out_grad)
    ]

    def trade(value, distance):
        return lax.ppermute(value, "seq", [(i, i ^ distance) for i in range(count)])

    def run(kernel, out, operands, after):
        return call(kernel, out, operands, after, name=(kernel.func if hasattr(kernel, "func") else kernel).__name__)

    part_eo, local_em, start_o = states_first(square, sources)
    start_in = trade(start_o, 1)
    part_em, start = states_mine(square, local_em, (start_o,))
    after = (start,)
    if square:
        (sent,) = run(row_first_kernel, [PIECE], (start, start_in), ())
        row_first = trade(sent, 2)
        after = (sent,)

    part_lo, part_lm, rest_o, rest = states_second(square, sources, after)
    rest_in = trade(rest_o, 1)
    sums_e, sums_l = (start, start_in), (rest, rest_in)
    partials_lo = within(scale, part_lo[:4], (rest_o,))
    after = (partials_lo[0],)
    if square:
        (sent,) = run(row_second_kernel, [PIECE], sums_l, after)
        row_second = trade(sent, 2)
        partials_lm = within(scale, part_lm[:4], (sent,), range(GROUP // 4))
        (sent,) = run(column_first_kernel, [PIECE], (*sums_l, row_first), (partials_lm[0],))
        column_first = trade(sent, 4)
        after = (sent,)
    else:
        partials_lm = within(scale, part_lm[:4], after, range(GROUP // 4))

    part_eo, part_em, later_o, later = states_other(square, sources, part_eo, part_em, after)
    later_in = trade(later_o, 1)
    sums_b = (later, later_in)
    partials_lm = within(scale, part_lm[:4], (later_o,), range(GROUP // 4, GROUP // 2), partials_lm)
    partials_eo = within(scale, part_eo[:4], (partials_lm[0],))
    if square:
        (sent,) = run(column_second_kernel, [PIECE], (*sums_e, row_second), (partials_eo[0],))
        column_second = trade(sent, 4)
        (sent,) = run(row_third_kernel, [PIECE], (*sums_b, column_first), (sent,))
        row_third = trade(sent, 2)
        arrived = (row_first, row_second, column_first)
        out = [state_of(GROUP), pltpu.VMEM((3, GROUP, HEAD_DIM, HEAD_DIM), jnp.float32), PIECE]
        own_e, other_e, own_prefix = run(first_states_kernel, out, (*sums_e, *sums_b, *sums_l, *arrived), (sent,))
    else:
        turns = range(1, count // 2)
        arrived = []
        sums = (*sums_e, *sums_b, *sums_l)
        for group in range(2):
            kernel = functools.partial(join_kernel, turns, group)
            sent = run(kernel, [PIECE] * len(turns), sums, (partials_eo[0],))
            arrived.append([trade(value, 2 * turn) for turn, value in zip(turns, sent, strict=True)])
        kernel = functools.partial(combine_kernel, turns, 0)
        own_e, other_e = run(kernel, STATES, (*sums, *arrived[0]), ())

    other_e = trade(other_e, 1)
    partials_em = within(scale, part_em[:4], (own_e,))
    parts = [(True, part_em[:4], partials_em, own_e, part_em[4:]), (False, part_eo[:4], partials_eo, other_e, part_eo[4:])]
    ahead = ()
    if square:
        ahead = (
            (part_lm[3], partials_lm[0], own_prefix, part_lm[4]),
            (part_lo[3], partials_lo[0], other_e, part_lo[4]),
        )
    done = finish(scale, square, 0, parts, (), ahead)

    after = (pltpu.with_memory_space_constraint(done[0], pltpu.HBM),)
    if square:
        arrived = (row_first, row_third, column_second)
        own_l, other_l = run(second_states_kernel, STATES, (*sums_l, *arrived), after)
    else:
        kernel = functools.partial(combine_kernel, turns, 1)
        own_l, other_l = run(kernel, STATES, (*sums, *arrived[1]), after)
    other_l = trade(other_l, 1)
    done = finish(scale, square, 1, [(True, part_lm[:4], partials_lm, own_l, part_lm[4:])], done)
    return tuple(finish(scale, square, 1, [(False, part_lo[:4], partials_lo, other_l, part_lo[4:])], done))


def solution(mesh):
    placed = P(("lists", "seq"), None)
    return jax.shard_map(
        on_device,
        mesh=mesh,
        in_specs=(placed,) * 4,
        out_specs=(placed,) * 3,
        check_vma=False,
    )
```

```python
import functools

import jax
import jax.numpy as jnp
from jax import lax
from jax.experimental import pallas as pl
from jax.experimental.pallas import tpu as pltpu
from jax.sharding import PartitionSpec as P

HEADS = 16
HEAD_DIM = 128
HALF = HEADS // 2
COLUMNS = HALF * HEAD_DIM
GROUP = HALF // 2
SUB = 256
PARTIAL = jnp.float32

TN = (((0,), (0,)), ((), ()))
NT = (((1,), (1,)), ((), ()))
NN = (((1,), (0,)), ((), ()))

IN_VMEM = pl.BlockSpec(memory_space=pltpu.VMEM)
ANYWHERE = pl.BlockSpec(memory_space=pl.ANY)
SHORT = pl.CostEstimate(flops=1000, bytes_accessed=1000, transcendentals=0)
LONG = pl.CostEstimate(flops=2 * 10**10, bytes_accessed=1000, transcendentals=0)


def dot(left, right, dims):
    return lax.dot_general(left, right, dims, preferred_element_type=jnp.float32)


def state_of(heads):
    return pltpu.VMEM((2, heads, HEAD_DIM, HEAD_DIM), jnp.float32)


def head_columns(head):
    return pl.ds(head * HEAD_DIM, HEAD_DIM)


def my_core():
    return lax.rem(lax.axis_index("seq"), 2)


def my_pair():
    return lax.div(lax.axis_index("seq"), 2)


def first_column(square, mine, group):
    half = my_core() if mine else 1 - my_core()
    if square:
        pair = my_pair()
        group = jnp.where((pair == 1) | (pair == 2), 1 - group, group)
    return half * COLUMNS + group * (GROUP * HEAD_DIM)


def my_row(square):
    return lax.div(my_pair(), 2) if square else jnp.int32(0)


PIECE = pltpu.VMEM((GROUP, HEAD_DIM, HEAD_DIM), jnp.float32)
STATES = [state_of(GROUP)] * 2


def call(kernel, out, operands, after=(), scratch=(), cost=SHORT, limit=3, name=None):
    return pl.pallas_call(
        kernel,
        out_shape=out,
        in_specs=[IN_VMEM] * len(operands) + [ANYWHERE] * len(after),
        out_specs=[IN_VMEM] * len(out),
        scratch_shapes=list(scratch),
        compiler_params=pltpu.CompilerParams(vmem_limit_bytes=limit << 20),
        cost_estimate=cost,
        name=name,
    )(*operands, *after)


KINDS = ((1, 2), (0, 3))


def read(square, mine, group, kind, sources, local, sems):
    width = GROUP * HEAD_DIM
    at = pl.ds(pl.multiple_of(first_column(square, mine, group), width), width)
    return [pltpu.make_async_copy(sources[i].at[:, at], local[i], sems.at[i]) for i in KINDS[kind]]


def start_all(copies):
    for copy in copies:
        copy.start()


def sum_kind(kind, copies, local, sums, early, late):
    for copy in copies:
        copy.wait()
    q, k, v, o = local
    left, right = ((k, v), (q, o))[kind]
    subs = q.shape[0] // SUB
    order = list(range(subs)) if kind == 0 else list(range(subs - 1, -1, -1))
    for head in range(GROUP):
        at = head_columns(head)
        total = None
        for sub in order:
            span = pl.ds(sub * SUB, SUB)
            part = dot(left[span, at], right[span, at], TN)
            total = part if total is None else total + part
            if sub != order[-1]:
                if kind == 0:
                    early[head, sub] = total
                else:
                    late[head, sub - 1] = total
        sums[head] = total


def work_inside(scale, local, outs, pairs):
    (q, k, v, o), (dq, dk, dv) = local, outs
    rows = q.shape[0]
    part = SUB // 2
    at_row = lax.broadcasted_iota(jnp.int32, (SUB, SUB), 0)
    at_column = lax.broadcasted_iota(jnp.int32, (SUB, SUB), 1)
    lower = at_row >= at_column
    upper = at_row <= at_column
    nothing = jnp.zeros((part, HEAD_DIM), jnp.bfloat16)

    def weights_of(unit):
        pair, sub = unit
        span = pl.ds(sub * SUB, SUB)
        weights = []
        for head in (2 * pair, 2 * pair + 1):
            at = head_columns(head)
            grads = jnp.where(lower, scale * dot(o[span, at], v[span, at], NT), 0.0).astype(jnp.bfloat16)
            forward = jnp.where(upper, scale * dot(k[span, at], q[span, at], NT), 0.0).astype(jnp.bfloat16)
            weights.append((grads, grads.T, forward))
        return weights

    def side_by_side(weights, rows):
        left = jnp.concatenate([rows[0], nothing], axis=1)
        right = jnp.concatenate([nothing, rows[1]], axis=1)
        product = dot(jnp.concatenate(weights, axis=1), jnp.concatenate([left, right], axis=0), NN)
        return product[:, :HEAD_DIM], product[:, HEAD_DIM:]

    def lower_product(weights, rows):
        first = side_by_side([w[:part, :part] for w in weights], [r[:part] for r in rows])
        return [
            jnp.concatenate([top, dot(w[part:], r, NN)], axis=0) for top, w, r in zip(first, weights, rows, strict=True)
        ]

    def upper_product(weights, rows):
        last = side_by_side([w[part:, part:] for w in weights], [r[part:] for r in rows])
        return [
            jnp.concatenate([dot(w[:part], r, NN), below], axis=0) for below, w, r in zip(last, weights, rows, strict=True)
        ]

    units = [(pair, sub) for pair in pairs for sub in range(rows // SUB)]
    ahead = weights_of(units[0])
    for number, (pair, sub) in enumerate(units):
        grads, grads_t, forward = zip(*ahead, strict=True)
        if number + 1 < len(units):
            ahead = weights_of(units[number + 1])
        span = pl.ds(sub * SUB, SUB)
        places = [head_columns(2 * pair), head_columns(2 * pair + 1)]
        for product, weights, source, out in (
            (lower_product, grads, k, dq),
            (upper_product, grads_t, q, dk),
            (upper_product, forward, o, dv),
        ):
            for at, piece in zip(places, product(weights, [source[span, at] for at in places]), strict=True):
                out[span, at] = piece.astype(PARTIAL)


def part_shapes(rows):
    inner = pltpu.VMEM((GROUP, rows // SUB - 1, HEAD_DIM, HEAD_DIM), jnp.float32)
    return [pltpu.VMEM((rows, GROUP * HEAD_DIM), jnp.bfloat16)] * 4 + [inner] * 2


def states_first_kernel(square, *refs):
    sources, part, local, sums, sems = refs[:4], refs[4:10], refs[10:14], refs[14], refs[15]
    row = my_row(square)
    for kind in range(2):
        copies = read(square, False, 0, kind, sources, part[:4], sems.at[0])
        behind = read(square, True, 0, kind, sources, local, sems.at[1])

        @pl.when(row == kind)
        def _():
            start_all(copies)
            start_all(behind)
            sum_kind(kind, copies, part[:4], sums, *part[4:])
            for copy in behind:
                copy.wait()


def states_first(square, sources):
    part = part_shapes(sources[0].shape[0])
    out = part + part[:4] + [PIECE]
    result = pl.pallas_call(
        functools.partial(states_first_kernel, square),
        out_shape=out,
        in_specs=[ANYWHERE] * 4,
        out_specs=[IN_VMEM] * len(out),
        scratch_shapes=[pltpu.SemaphoreType.DMA((2, 4))],
        compiler_params=pltpu.CompilerParams(vmem_limit_bytes=2 << 20),
        cost_estimate=LONG,
        name="states_first",
    )(*sources)
    return result[:6], result[6:10], result[10]


def states_mine_kernel(square, *refs):
    local, inner, sums = refs[:4], refs[-3:-1], refs[-1]
    row = my_row(square)
    for kind in range(2):

        @pl.when(row == kind)
        def _():
            sum_kind(kind, (), local, sums, *inner)


def states_mine(square, local, after):
    inner = part_shapes(local[0].shape[0])[4:]
    out = [*inner, PIECE]
    kernel = functools.partial(states_mine_kernel, square)
    *inner, sums = call(kernel, out, local, after, cost=LONG, limit=2, name="states_mine")
    return [*local, *inner], sums


def states_second_kernel(square, *refs):
    sources, parts, sums, sems = refs[:4], (refs[-15:-9], refs[-9:-3]), refs[-3:-1], refs[-1]
    copies = {}
    for mine in range(2):
        for kind in range(2):
            copies[mine, kind] = read(square, bool(mine), 1, kind, sources, parts[mine][:4], sems.at[mine])
            start_all(copies[mine, kind])
    for mine in range(2):
        for kind in range(2):
            sum_kind(kind, copies[mine, kind], parts[mine][:4], sums[mine].at[kind], *parts[mine][4:])


def states_second(square, sources, after):
    out = part_shapes(sources[0].shape[0]) * 2 + [state_of(GROUP)] * 2
    result = pl.pallas_call(
        functools.partial(states_second_kernel, square),
        out_shape=out,
        in_specs=[ANYWHERE] * (4 + len(after)),
        out_specs=[IN_VMEM] * len(out),
        scratch_shapes=[pltpu.SemaphoreType.DMA((2, 4))],
        compiler_params=pltpu.CompilerParams(vmem_limit_bytes=2 << 20),
        cost_estimate=LONG,
        name="states_second",
    )(*sources, *after)
    return result[:6], result[6:12], *result[12:]


def states_other_kernel(square, *refs):
    sources, along, parts, sems = refs[:4], refs[16], (refs[-15:-9], refs[-9:-3]), refs[-1]
    sums = refs[-3].at[0], refs[-2]
    refs[-3][1] = along[...]
    row = my_row(square)
    copies = {}
    for mine in range(2):
        for kind in range(2):
            copies[mine, kind] = read(square, bool(mine), 0, kind, sources, parts[mine][:4], sems.at[mine])
    for kind in range(2):

        @pl.when(row != kind)
        def _():
            for mine in range(2):
                start_all(copies[mine, kind])
            for mine in range(2):
                sum_kind(kind, copies[mine, kind], parts[mine][:4], sums[mine], *parts[mine][4:])


def states_other(square, sources, other, mine, along, after):
    out = part_shapes(sources[0].shape[0]) * 2 + [state_of(GROUP), PIECE]
    result = pl.pallas_call(
        functools.partial(states_other_kernel, square),
        out_shape=out,
        in_specs=[ANYWHERE] * 4 + [IN_VMEM] * 13 + [ANYWHERE] * len(after),
        out_specs=[IN_VMEM] * len(out),
        scratch_shapes=[pltpu.SemaphoreType.DMA((2, 4))],
        input_output_aliases={4 + i: i for i in range(12)},
        compiler_params=pltpu.CompilerParams(vmem_limit_bytes=2 << 20),
        cost_estimate=LONG,
        name="states_other",
    )(*sources, *other, *mine, along, *after)
    return result[:6], result[6:12], *result[12:]


def within_kernel(scale, pairs, *refs):
    work_inside(scale, refs[:4], refs[-3:], pairs)


def within(scale, local, after, pairs=range(GROUP // 2), into=()):
    out = [pltpu.VMEM(local[0].shape, PARTIAL)] * 3
    return pl.pallas_call(
        functools.partial(within_kernel, scale, tuple(pairs)),
        out_shape=out,
        in_specs=[IN_VMEM] * (4 + len(into)) + [ANYWHERE] * len(after),
        out_specs=[IN_VMEM] * 3,
        input_output_aliases={4 + i: i for i in range(len(into))},
        compiler_params=pltpu.CompilerParams(vmem_limit_bytes=3 << 20),
        cost_estimate=LONG,
        name="within",
    )(*local, *into, *after)


def first_group(square, head, start, later):
    upper = my_row(square) == 0
    one, other = start[head], later[head]
    return jnp.where(upper, one, other), jnp.where(upper, other, one)


def second_group(head, rest):
    return rest[0, head], rest[1, head]


def settle(head, prefix, suffix, sums, sums_in, own, other):
    second = my_core() == 1
    own[0, head] = prefix + jnp.where(second, sums_in[0], 0.0)
    own[1, head] = suffix + jnp.where(second, 0.0, sums_in[1])
    other[0, head] = prefix + jnp.where(second, 0.0, sums[0])
    other[1, head] = suffix + jnp.where(second, sums[1], 0.0)


def comes_earlier(turn):
    pair = my_pair()
    return jnp.bitwise_xor(pair, turn) < pair


def sums_of_group(group, head, start, start_in, later, later_in, rest, rest_in):
    if group == 0:
        return first_group(False, head, start, later), first_group(False, head, start_in, later_in.at[0])
    return second_group(head, rest), second_group(head, rest_in)


def join_kernel(turns, group, *refs):
    for head in range(GROUP):
        sums, sums_in = sums_of_group(group, head, *refs[:6])
        for turn, out in zip(turns, refs[-len(turns) :], strict=True):
            out[head] = jnp.where(comes_earlier(turn), sums[1] + sums_in[1], sums[0] + sums_in[0])


def combine_kernel(turns, group, *refs):
    received = refs[6 : 6 + len(turns)]
    for head in range(GROUP):
        sums, sums_in = sums_of_group(group, head, *refs[:6])
        prefix = jnp.zeros((HEAD_DIM, HEAD_DIM), jnp.float32)
        suffix = jnp.zeros((HEAD_DIM, HEAD_DIM), jnp.float32)
        for turn, value in zip(turns, received, strict=True):
            earlier = comes_earlier(turn)
            prefix = prefix + jnp.where(earlier, value[head], 0.0)
            suffix = suffix + jnp.where(earlier, 0.0, value[head])
        settle(head, prefix, suffix, sums, sums_in, *refs[-2:])


def row_first_kernel(start, start_in, *refs):
    for head in range(GROUP):
        refs[-1][head] = start[head] + start_in[head]


def row_second_kernel(rest, rest_in, *refs):
    kind = lax.rem(my_pair(), 2)
    for head in range(GROUP):
        refs[-1][head] = rest[kind, head] + rest_in[kind, head]


def column_first_kernel(rest, rest_in, from_row, *refs):
    sent, own_prefix, other_prefix = refs[-3:]
    kind = my_row(True)
    second = my_core() == 1
    for head in range(GROUP):
        sent[head] = rest[kind, head] + rest_in[kind, head] + from_row[head]
        prefix = jnp.where(my_pair() == 1, from_row[head], 0.0)
        own_prefix[head] = prefix + jnp.where(second, rest_in[0, head], 0.0)
        other_prefix[head] = prefix + jnp.where(second, 0.0, rest[0, head])


def column_second_kernel(start, start_in, from_row, *refs):
    for head in range(GROUP):
        refs[-1][head] = start[head] + start_in[head] + from_row[head]


def row_third_kernel(later, later_in, from_column, *refs):
    pair = my_pair()
    outer = (pair == 0) | (pair == 3)
    for head in range(GROUP):
        refs[-1][head] = jnp.where(outer, from_column[head], later[head] + later_in[0, head])


def first_states_kernel(start, start_in, later, later_in, row_second, column_first, *refs):
    pair = my_pair()
    below, right = pair >= 2, lax.rem(pair, 2) == 1
    for head in range(GROUP):
        row, column = row_second[head], column_first[head]
        prefix = jnp.where(right, row, 0.0) + jnp.where(below, column, 0.0)
        suffix = jnp.where(right, 0.0, row) + jnp.where(below, 0.0, column)
        sums, sums_in = first_group(True, head, start, later), first_group(True, head, start_in, later_in.at[0])
        settle(head, prefix, suffix, sums, sums_in, *refs[-2:])


def second_states_kernel(rest, rest_in, row_first, row_third, column_second, *refs):
    pair = my_pair()
    below, outer = pair >= 2, (pair == 0) | (pair == 3)
    for head in range(GROUP):
        passed = row_third[head] + jnp.where(outer, column_second[head], 0.0)
        prefix = jnp.where(pair == 1, row_first[head], 0.0) + jnp.where(below, passed, 0.0)
        suffix = jnp.where(pair == 2, row_first[head], 0.0) + jnp.where(below, 0.0, passed)
        settle(head, prefix, suffix, second_group(head, rest), second_group(head, rest_in), *refs[-2:])


def add_state(scale, head, partial, rows, states, inner, dims, out, to):
    at = head_columns(head)
    subs = rows.shape[0] // SUB
    for sub in range(subs):
        span = pl.ds(sub * SUB, SUB)
        state = states[head]
        if dims[1] == 0:
            state = state + inner[head, sub - 1] if sub > 0 else state
        else:
            state = state + inner[head, sub] if sub < subs - 1 else state
        piece = partial[span, at] + scale * dot(rows[span, at], state.astype(jnp.bfloat16), dims[0])
        out[span, to] = piece.astype(jnp.bfloat16)


QUERY, KEY, VALUE = (NT, 0), (NT, 1), (NN, 1)


def finish_kernel(scale, square, group, halves, ahead, *refs):
    targets, staged, sems = refs[-7:-4], refs[-4:-1], refs[-1]
    row = my_row(square)

    def copies_of(i, number, which, first, heads):
        mine, at_group = halves[number % len(halves)], 1 if number >= len(halves) else group
        width = heads * HEAD_DIM
        column = first_column(square, mine, at_group) + first * HEAD_DIM
        return pltpu.make_async_copy(
            staged[i].at[:, pl.ds((number * GROUP + first) * HEAD_DIM, width)],
            targets[i].at[:, pl.ds(pl.multiple_of(column, HEAD_DIM), width)],
            sems.at[number, which, i],
        )

    def run(i, number, copies, partial, rows, states, inner, dims):
        for head in range(GROUP):
            to = head_columns(number * GROUP + head)
            add_state(scale, head, partial, rows, states, inner, dims, staged[i], to)
            if head % 2 == 1:
                copies[head // 2].start()

    def pieces(i, number):
        return [copies_of(i, number, which, 2 * which, 2) for which in range(GROUP // 2)]

    sometimes, always = [], []
    for number in range(len(halves)):
        k, v, o, dq, dk, dv, state, early, late = refs[9 * number : 9 * number + 9]
        query = pieces(0, number)
        if square and group == 1:
            sometimes += query

            @pl.when(row == 1)
            def _():
                run(0, number, query, dq, o, state.at[0], early, QUERY)
        else:
            always += query
            run(0, number, query, dq, o, state.at[0], early, QUERY)
        for i, arguments in ((1, (dk, v, state.at[1], late, KEY)), (2, (dv, k, state.at[1], late, VALUE))):
            copies = pieces(i, number)
            always += copies
            run(i, number, copies, *arguments)
    rest = refs[9 * len(halves) :]
    for n in range(ahead):
        number = len(halves) + n
        o, dq, prefix, early = rest[4 * n : 4 * n + 4]
        prefix = prefix if n == 0 else prefix.at[1]
        query = pieces(0, number)
        sometimes += query

        @pl.when(row == 0)
        def _():
            run(0, number, query, dq, o, prefix, early, QUERY)

    for copy in always:
        copy.wait()
    if sometimes:

        @pl.when(row == (0 if ahead else 1))
        def _():
            for copy in sometimes:
                copy.wait()


def finish(scale, square, group, parts, before, ahead=()):
    rows = parts[0][1][0].shape[0]
    out = [jax.ShapeDtypeStruct((rows, HEADS * HEAD_DIM), jnp.bfloat16)] * 3
    halves = tuple(part[0] for part in parts)
    operands = []
    for _, local, partials, state, inner in parts:
        operands += [*local[1:], *partials, state, *inner]
    for arrays in ahead:
        operands += arrays
    widths = [(len(parts) + extra) * GROUP * HEAD_DIM for extra in (len(ahead), 0, 0)]
    return pl.pallas_call(
        functools.partial(finish_kernel, scale, square, group, halves, len(ahead)),
        out_shape=out,
        in_specs=[IN_VMEM] * len(operands) + [ANYWHERE] * len(before),
        out_specs=[ANYWHERE] * 3,
        scratch_shapes=[pltpu.VMEM((rows, width), jnp.bfloat16) for width in widths]
        + [pltpu.SemaphoreType.DMA((len(parts) + len(ahead), GROUP // 2, 3))],
        input_output_aliases={len(operands) + i: i for i in range(len(before))},
        compiler_params=pltpu.CompilerParams(vmem_limit_bytes=(2 + 3 * len(parts) + len(ahead)) << 20),
        cost_estimate=LONG,
        name="finish",
    )(*operands, *before)


def on_device(queries, key_rows, value_rows, out_grad):
    count = lax.axis_size("seq")
    square = count == 8
    scale = (HEAD_DIM * queries.shape[0] * count) ** -0.5
    sources = [
        pltpu.with_memory_space_constraint(array, pltpu.HBM) for array in (queries, key_rows, value_rows, out_grad)
    ]

    def trade(value, distance):
        return lax.ppermute(value, "seq", [(i, i ^ distance) for i in range(count)])

    def run(kernel, out, operands, after):
        return call(kernel, out, operands, after, name=(kernel.func if hasattr(kernel, "func") else kernel).__name__)

    part_eo, local_em, start_o = states_first(square, sources)
    start_in = trade(start_o, 1)
    part_em, start = states_mine(square, local_em, (start_o,))
    after = (start,)
    if square:
        (sent,) = run(row_first_kernel, [PIECE], (start, start_in), ())
        row_first = trade(sent, 2)
        after = (sent,)

    part_lo, part_lm, rest_o, rest = states_second(square, sources, after)
    rest_in = trade(rest_o, 1)
    sums_e, sums_l = (start, start_in), (rest, rest_in)
    partials_lo = within(scale, part_lo[:4], (rest_o,))
    after = (partials_lo[0],)
    if square:
        (sent,) = run(row_second_kernel, [PIECE], sums_l, after)
        row_second = trade(sent, 2)
        partials_lm = within(scale, part_lm[:4], (sent,), range(GROUP // 4))
        sent, own_prefix, along = run(column_first_kernel, [PIECE] * 3, (*sums_l, row_first), (partials_lm[0],))
        column_first = trade(sent, 4)
        after = (sent,)
    else:
        partials_lm = within(scale, part_lm[:4], after, range(GROUP // 4))
        along = start

    part_eo, part_em, later_o, later = states_other(square, sources, part_eo, part_em, along, after)
    later_in = trade(later_o, 1)
    sums_b = (later, later_in)
    partials_lm = within(scale, part_lm[:4], (later_o,), range(GROUP // 4, GROUP // 2), partials_lm)
    partials_eo = within(scale, part_eo[:4], (partials_lm[0],))
    if square:
        (sent,) = run(column_second_kernel, [PIECE], (*sums_e, row_second), (partials_eo[0],))
        column_second = trade(sent, 4)
        (sent,) = run(row_third_kernel, [PIECE], (*sums_b, column_first), (sent,))
        row_third = trade(sent, 2)
        arrived = (row_second, column_first)
        own_e, other_e = run(first_states_kernel, STATES, (*sums_e, *sums_b, *arrived), (sent,))
    else:
        turns = range(1, count // 2)
        arrived = []
        sums = (*sums_e, *sums_b, *sums_l)
        for group in range(2):
            kernel = functools.partial(join_kernel, turns, group)
            sent = run(kernel, [PIECE] * len(turns), sums, (partials_eo[0],))
            arrived.append([trade(value, 2 * turn) for turn, value in zip(turns, sent, strict=True)])
        kernel = functools.partial(combine_kernel, turns, 0)
        own_e, other_e = run(kernel, STATES, (*sums, *arrived[0]), ())

    other_e = trade(other_e, 1)
    partials_em = within(scale, part_em[:4], (own_e,))
    parts = [(True, part_em[:4], partials_em, own_e, part_em[4:]), (False, part_eo[:4], partials_eo, other_e, part_eo[4:])]
    ahead = ()
    if square:
        ahead = (
            (part_lm[3], partials_lm[0], own_prefix, part_lm[4]),
            (part_lo[3], partials_lo[0], later_in, part_lo[4]),
        )
    done = finish(scale, square, 0, parts, (), ahead)

    after = (pltpu.with_memory_space_constraint(done[0], pltpu.HBM),)
    if square:
        arrived = (row_first, row_third, column_second)
        own_l, other_l = run(second_states_kernel, STATES, (*sums_l, *arrived), after)
    else:
        kernel = functools.partial(combine_kernel, turns, 1)
        own_l, other_l = run(kernel, STATES, (*sums, *arrived[1]), after)
    other_l = trade(other_l, 1)
    done = finish(scale, square, 1, [(True, part_lm[:4], partials_lm, own_l, part_lm[4:])], done)
    return tuple(finish(scale, square, 1, [(False, part_lo[:4], partials_lo, other_l, part_lo[4:])], done))


def solution(mesh):
    placed = P(("lists", "seq"), None)
    return jax.shard_map(
        on_device,
        mesh=mesh,
        in_specs=(placed,) * 4,
        out_specs=(placed,) * 3,
        check_vma=False,
    )
```

```python
import functools

import jax
import jax.numpy as jnp
from jax import lax
from jax.experimental import pallas as pl
from jax.experimental.pallas import tpu as pltpu
from jax.sharding import PartitionSpec as P

HEADS = 16
HEAD_DIM = 128
HALF = HEADS // 2
COLUMNS = HALF * HEAD_DIM
GROUP = HALF // 2
SUB = 256
PARTIAL = jnp.bfloat16

TN = (((0,), (0,)), ((), ()))
NT = (((1,), (1,)), ((), ()))
NN = (((1,), (0,)), ((), ()))

IN_VMEM = pl.BlockSpec(memory_space=pltpu.VMEM)
ANYWHERE = pl.BlockSpec(memory_space=pl.ANY)
SHORT = pl.CostEstimate(flops=1000, bytes_accessed=1000, transcendentals=0)
LONG = pl.CostEstimate(flops=2 * 10**10, bytes_accessed=1000, transcendentals=0)


def dot(left, right, dims):
    return lax.dot_general(left, right, dims, preferred_element_type=jnp.float32)


def state_of(heads):
    return pltpu.VMEM((2, heads, HEAD_DIM, HEAD_DIM), jnp.float32)


def head_columns(head):
    return pl.ds(head * HEAD_DIM, HEAD_DIM)


def my_core():
    return lax.rem(lax.axis_index("seq"), 2)


def my_pair():
    return lax.div(lax.axis_index("seq"), 2)


def first_column(square, mine, group):
    half = my_core() if mine else 1 - my_core()
    if square:
        pair = my_pair()
        group = jnp.where((pair == 1) | (pair == 2), 1 - group, group)
    return half * COLUMNS + group * (GROUP * HEAD_DIM)


def my_row(square):
    return lax.div(my_pair(), 2) if square else jnp.int32(0)


PIECE = pltpu.VMEM((GROUP, HEAD_DIM, HEAD_DIM), jnp.float32)
STATES = [state_of(GROUP)] * 2


def call(kernel, out, operands, after=(), scratch=(), cost=SHORT, limit=3, name=None):
    return pl.pallas_call(
        kernel,
        out_shape=out,
        in_specs=[IN_VMEM] * len(operands) + [ANYWHERE] * len(after),
        out_specs=[IN_VMEM] * len(out),
        scratch_shapes=list(scratch),
        compiler_params=pltpu.CompilerParams(vmem_limit_bytes=limit << 20),
        cost_estimate=cost,
        name=name,
    )(*operands, *after)


KINDS = ((1, 2), (0, 3))


def read(square, mine, group, kind, sources, local, sems):
    width = GROUP * HEAD_DIM
    at = pl.ds(pl.multiple_of(first_column(square, mine, group), width), width)
    return [pltpu.make_async_copy(sources[i].at[:, at], local[i], sems.at[i]) for i in KINDS[kind]]


def start_all(copies):
    for copy in copies:
        copy.start()


def sum_kind(kind, copies, local, sums, early, late):
    for copy in copies:
        copy.wait()
    q, k, v, o = local
    left, right = ((k, v), (q, o))[kind]
    subs = q.shape[0] // SUB
    order = list(range(subs)) if kind == 0 else list(range(subs - 1, -1, -1))
    for head in range(GROUP):
        at = head_columns(head)
        total = None
        for sub in order:
            span = pl.ds(sub * SUB, SUB)
            part = dot(left[span, at], right[span, at], TN)
            total = part if total is None else total + part
            if sub != order[-1]:
                if kind == 0:
                    early[head, sub] = total
                else:
                    late[head, sub - 1] = total
        sums[head] = total


def work_inside(scale, local, outs, pairs):
    (q, k, v, o), (dq, dk, dv) = local, outs
    rows = q.shape[0]
    part = SUB // 2
    at_row = lax.broadcasted_iota(jnp.int32, (SUB, SUB), 0)
    at_column = lax.broadcasted_iota(jnp.int32, (SUB, SUB), 1)
    lower = at_row >= at_column
    upper = at_row <= at_column
    nothing = jnp.zeros((part, HEAD_DIM), jnp.bfloat16)

    def weights_of(unit):
        pair, sub = unit
        span = pl.ds(sub * SUB, SUB)
        weights = []
        for head in (2 * pair, 2 * pair + 1):
            at = head_columns(head)
            grads = jnp.where(lower, scale * dot(o[span, at], v[span, at], NT), 0.0).astype(jnp.bfloat16)
            forward = jnp.where(upper, scale * dot(k[span, at], q[span, at], NT), 0.0).astype(jnp.bfloat16)
            weights.append((grads, grads.T, forward))
        return weights

    def side_by_side(weights, rows):
        left = jnp.concatenate([rows[0], nothing], axis=1)
        right = jnp.concatenate([nothing, rows[1]], axis=1)
        product = dot(jnp.concatenate(weights, axis=1), jnp.concatenate([left, right], axis=0), NN)
        return product[:, :HEAD_DIM], product[:, HEAD_DIM:]

    def lower_product(weights, rows):
        first = side_by_side([w[:part, :part] for w in weights], [r[:part] for r in rows])
        return [
            jnp.concatenate([top, dot(w[part:], r, NN)], axis=0) for top, w, r in zip(first, weights, rows, strict=True)
        ]

    def upper_product(weights, rows):
        last = side_by_side([w[part:, part:] for w in weights], [r[part:] for r in rows])
        return [
            jnp.concatenate([dot(w[:part], r, NN), below], axis=0) for below, w, r in zip(last, weights, rows, strict=True)
        ]

    units = [(pair, sub) for pair in pairs for sub in range(rows // SUB)]
    ahead = weights_of(units[0])
    for number, (pair, sub) in enumerate(units):
        grads, grads_t, forward = zip(*ahead, strict=True)
        if number + 1 < len(units):
            ahead = weights_of(units[number + 1])
        span = pl.ds(sub * SUB, SUB)
        places = [head_columns(2 * pair), head_columns(2 * pair + 1)]
        for product, weights, source, out in (
            (lower_product, grads, k, dq),
            (upper_product, grads_t, q, dk),
            (upper_product, forward, o, dv),
        ):
            for at, piece in zip(places, product(weights, [source[span, at] for at in places]), strict=True):
                out[span, at] = piece.astype(PARTIAL)


def part_shapes(rows):
    inner = pltpu.VMEM((GROUP, rows // SUB - 1, HEAD_DIM, HEAD_DIM), jnp.float32)
    return [pltpu.VMEM((rows, GROUP * HEAD_DIM), jnp.bfloat16)] * 4 + [inner] * 2


def states_first_kernel(square, *refs):
    sources, part, local, sums, sems = refs[:4], refs[4:10], refs[10:14], refs[14], refs[15]
    row = my_row(square)
    for kind in range(2):
        copies = read(square, False, 0, kind, sources, part[:4], sems.at[0])
        behind = read(square, True, 0, kind, sources, local, sems.at[1])

        @pl.when(row == kind)
        def _():
            start_all(copies)
            start_all(behind)
            sum_kind(kind, copies, part[:4], sums, *part[4:])
            for copy in behind:
                copy.wait()


def states_first(square, sources):
    part = part_shapes(sources[0].shape[0])
    out = part + part[:4] + [PIECE]
    result = pl.pallas_call(
        functools.partial(states_first_kernel, square),
        out_shape=out,
        in_specs=[ANYWHERE] * 4,
        out_specs=[IN_VMEM] * len(out),
        scratch_shapes=[pltpu.SemaphoreType.DMA((2, 4))],
        compiler_params=pltpu.CompilerParams(vmem_limit_bytes=2 << 20),
        cost_estimate=LONG,
        name="states_first",
    )(*sources)
    return result[:6], result[6:10], result[10]


def states_mine_kernel(square, *refs):
    local, inner, sums = refs[:4], refs[-3:-1], refs[-1]
    row = my_row(square)
    for kind in range(2):

        @pl.when(row == kind)
        def _():
            sum_kind(kind, (), local, sums, *inner)


def states_mine(square, local, after):
    inner = part_shapes(local[0].shape[0])[4:]
    out = [*inner, PIECE]
    kernel = functools.partial(states_mine_kernel, square)
    *inner, sums = call(kernel, out, local, after, cost=LONG, limit=2, name="states_mine")
    return [*local, *inner], sums


def states_second_kernel(square, *refs):
    sources, parts, sums, sems = refs[:4], (refs[-15:-9], refs[-9:-3]), refs[-3:-1], refs[-1]
    copies = {}
    for mine in range(2):
        for kind in range(2):
            copies[mine, kind] = read(square, bool(mine), 1, kind, sources, parts[mine][:4], sems.at[mine])
            start_all(copies[mine, kind])
    for mine in range(2):
        for kind in range(2):
            sum_kind(kind, copies[mine, kind], parts[mine][:4], sums[mine].at[kind], *parts[mine][4:])


def states_second(square, sources, after):
    out = part_shapes(sources[0].shape[0]) * 2 + [state_of(GROUP)] * 2
    result = pl.pallas_call(
        functools.partial(states_second_kernel, square),
        out_shape=out,
        in_specs=[ANYWHERE] * (4 + len(after)),
        out_specs=[IN_VMEM] * len(out),
        scratch_shapes=[pltpu.SemaphoreType.DMA((2, 4))],
        compiler_params=pltpu.CompilerParams(vmem_limit_bytes=2 << 20),
        cost_estimate=LONG,
        name="states_second",
    )(*sources, *after)
    return result[:6], result[6:12], *result[12:]


def states_other_kernel(square, *refs):
    sources, along, parts, sems = refs[:4], refs[16], (refs[-15:-9], refs[-9:-3]), refs[-1]
    sums = refs[-3].at[0], refs[-2]
    refs[-3][1] = along[...]
    row = my_row(square)
    copies = {}
    for mine in range(2):
        for kind in range(2):
            copies[mine, kind] = read(square, bool(mine), 0, kind, sources, parts[mine][:4], sems.at[mine])
    for kind in range(2):

        @pl.when(row != kind)
        def _():
            for mine in range(2):
                start_all(copies[mine, kind])
            for mine in range(2):
                sum_kind(kind, copies[mine, kind], parts[mine][:4], sums[mine], *parts[mine][4:])


def states_other(square, sources, other, mine, along, after):
    out = part_shapes(sources[0].shape[0]) * 2 + [state_of(GROUP), PIECE]
    result = pl.pallas_call(
        functools.partial(states_other_kernel, square),
        out_shape=out,
        in_specs=[ANYWHERE] * 4 + [IN_VMEM] * 13 + [ANYWHERE] * len(after),
        out_specs=[IN_VMEM] * len(out),
        scratch_shapes=[pltpu.SemaphoreType.DMA((2, 4))],
        input_output_aliases={4 + i: i for i in range(12)},
        compiler_params=pltpu.CompilerParams(vmem_limit_bytes=2 << 20),
        cost_estimate=LONG,
        name="states_other",
    )(*sources, *other, *mine, along, *after)
    return result[:6], result[6:12], *result[12:]


def within_kernel(scale, pairs, *refs):
    work_inside(scale, refs[:4], refs[-3:], pairs)


def within(scale, local, after, pairs=range(GROUP // 2), into=()):
    out = [pltpu.VMEM(local[0].shape, PARTIAL)] * 3
    return pl.pallas_call(
        functools.partial(within_kernel, scale, tuple(pairs)),
        out_shape=out,
        in_specs=[IN_VMEM] * (4 + len(into)) + [ANYWHERE] * len(after),
        out_specs=[IN_VMEM] * 3,
        input_output_aliases={4 + i: i for i in range(len(into))},
        compiler_params=pltpu.CompilerParams(vmem_limit_bytes=3 << 20),
        cost_estimate=LONG,
        name="within",
    )(*local, *into, *after)


def first_group(square, head, start, later):
    upper = my_row(square) == 0
    one, other = start[head], later[head]
    return jnp.where(upper, one, other), jnp.where(upper, other, one)


def second_group(head, rest):
    return rest[0, head], rest[1, head]


def settle(head, prefix, suffix, sums, sums_in, own, other):
    second = my_core() == 1
    own[0, head] = prefix + jnp.where(second, sums_in[0], 0.0)
    own[1, head] = suffix + jnp.where(second, 0.0, sums_in[1])
    other[0, head] = prefix + jnp.where(second, 0.0, sums[0])
    other[1, head] = suffix + jnp.where(second, sums[1], 0.0)


def comes_earlier(turn):
    pair = my_pair()
    return jnp.bitwise_xor(pair, turn) < pair


def sums_of_group(group, head, start, start_in, later, later_in, rest, rest_in):
    if group == 0:
        return first_group(False, head, start, later), first_group(False, head, start_in, later_in.at[0])
    return second_group(head, rest), second_group(head, rest_in)


def join_kernel(turns, group, *refs):
    for head in range(GROUP):
        sums, sums_in = sums_of_group(group, head, *refs[:6])
        for turn, out in zip(turns, refs[-len(turns) :], strict=True):
            out[head] = jnp.where(comes_earlier(turn), sums[1] + sums_in[1], sums[0] + sums_in[0])


def combine_kernel(turns, group, *refs):
    received = refs[6 : 6 + len(turns)]
    for head in range(GROUP):
        sums, sums_in = sums_of_group(group, head, *refs[:6])
        prefix = jnp.zeros((HEAD_DIM, HEAD_DIM), jnp.float32)
        suffix = jnp.zeros((HEAD_DIM, HEAD_DIM), jnp.float32)
        for turn, value in zip(turns, received, strict=True):
            earlier = comes_earlier(turn)
            prefix = prefix + jnp.where(earlier, value[head], 0.0)
            suffix = suffix + jnp.where(earlier, 0.0, value[head])
        settle(head, prefix, suffix, sums, sums_in, *refs[-2:])


def row_first_kernel(start, start_in, *refs):
    for head in range(GROUP):
        refs[-1][head] = start[head] + start_in[head]


def row_second_kernel(rest, rest_in, *refs):
    kind = lax.rem(my_pair(), 2)
    for head in range(GROUP):
        refs[-1][head] = rest[kind, head] + rest_in[kind, head]


def column_first_kernel(rest, rest_in, from_row, *refs):
    sent, own_prefix, other_prefix = refs[-3:]
    kind = my_row(True)
    second = my_core() == 1
    for head in range(GROUP):
        sent[head] = rest[kind, head] + rest_in[kind, head] + from_row[head]
        prefix = jnp.where(my_pair() == 1, from_row[head], 0.0)
        own_prefix[head] = prefix + jnp.where(second, rest_in[0, head], 0.0)
        other_prefix[head] = prefix + jnp.where(second, 0.0, rest[0, head])


def column_second_kernel(start, start_in, from_row, *refs):
    for head in range(GROUP):
        refs[-1][head] = start[head] + start_in[head] + from_row[head]


def row_third_kernel(later, later_in, from_column, *refs):
    pair = my_pair()
    outer = (pair == 0) | (pair == 3)
    for head in range(GROUP):
        refs[-1][head] = jnp.where(outer, from_column[head], later[head] + later_in[0, head])


def first_states_kernel(start, start_in, later, later_in, row_second, column_first, *refs):
    pair = my_pair()
    below, right = pair >= 2, lax.rem(pair, 2) == 1
    for head in range(GROUP):
        row, column = row_second[head], column_first[head]
        prefix = jnp.where(right, row, 0.0) + jnp.where(below, column, 0.0)
        suffix = jnp.where(right, 0.0, row) + jnp.where(below, 0.0, column)
        sums, sums_in = first_group(True, head, start, later), first_group(True, head, start_in, later_in.at[0])
        settle(head, prefix, suffix, sums, sums_in, *refs[-2:])


def second_states_kernel(rest, rest_in, row_first, row_third, column_second, *refs):
    pair = my_pair()
    below, outer = pair >= 2, (pair == 0) | (pair == 3)
    for head in range(GROUP):
        passed = row_third[head] + jnp.where(outer, column_second[head], 0.0)
        prefix = jnp.where(pair == 1, row_first[head], 0.0) + jnp.where(below, passed, 0.0)
        suffix = jnp.where(pair == 2, row_first[head], 0.0) + jnp.where(below, 0.0, passed)
        settle(head, prefix, suffix, second_group(head, rest), second_group(head, rest_in), *refs[-2:])


def add_state(scale, head, partial, rows, states, inner, dims, out, to):
    at = head_columns(head)
    subs = rows.shape[0] // SUB
    for sub in range(subs):
        span = pl.ds(sub * SUB, SUB)
        state = states[head]
        if dims[1] == 0:
            state = state + inner[head, sub - 1] if sub > 0 else state
        else:
            state = state + inner[head, sub] if sub < subs - 1 else state
        piece = partial[span, at] + scale * dot(rows[span, at], state.astype(jnp.bfloat16), dims[0])
        out[span, to] = piece.astype(jnp.bfloat16)


QUERY, KEY, VALUE = (NT, 0), (NT, 1), (NN, 1)


def finish_kernel(scale, square, group, halves, ahead, *refs):
    targets, staged, sems = refs[-7:-4], refs[-4:-1], refs[-1]
    row = my_row(square)

    def copies_of(i, number, which, first, heads):
        mine, at_group = halves[number % len(halves)], 1 if number >= len(halves) else group
        width = heads * HEAD_DIM
        column = first_column(square, mine, at_group) + first * HEAD_DIM
        return pltpu.make_async_copy(
            staged[i].at[:, pl.ds((number * GROUP + first) * HEAD_DIM, width)],
            targets[i].at[:, pl.ds(pl.multiple_of(column, HEAD_DIM), width)],
            sems.at[number, which, i],
        )

    def run(i, number, copies, partial, rows, states, inner, dims):
        for head in range(GROUP):
            to = head_columns(number * GROUP + head)
            add_state(scale, head, partial, rows, states, inner, dims, staged[i], to)
            if head % 2 == 1:
                copies[head // 2].start()

    def pieces(i, number):
        return [copies_of(i, number, which, 2 * which, 2) for which in range(GROUP // 2)]

    sometimes, always = [], []
    for number in range(len(halves)):
        k, v, o, dq, dk, dv, state, early, late = refs[9 * number : 9 * number + 9]
        query = pieces(0, number)
        if square and group == 1:
            sometimes += query

            @pl.when(row == 1)
            def _():
                run(0, number, query, dq, o, state.at[0], early, QUERY)
        else:
            always += query
            run(0, number, query, dq, o, state.at[0], early, QUERY)
        for i, arguments in ((1, (dk, v, state.at[1], late, KEY)), (2, (dv, k, state.at[1], late, VALUE))):
            copies = pieces(i, number)
            always += copies
            run(i, number, copies, *arguments)
    rest = refs[9 * len(halves) :]
    for n in range(ahead):
        number = len(halves) + n
        o, dq, prefix, early = rest[4 * n : 4 * n + 4]
        prefix = prefix if n == 0 else prefix.at[1]
        query = pieces(0, number)
        sometimes += query

        @pl.when(row == 0)
        def _():
            run(0, number, query, dq, o, prefix, early, QUERY)

    for copy in always:
        copy.wait()
    if sometimes:

        @pl.when(row == (0 if ahead else 1))
        def _():
            for copy in sometimes:
                copy.wait()


def finish(scale, square, group, parts, before, ahead=()):
    rows = parts[0][1][0].shape[0]
    out = [jax.ShapeDtypeStruct((rows, HEADS * HEAD_DIM), jnp.bfloat16)] * 3
    halves = tuple(part[0] for part in parts)
    operands = []
    for _, local, partials, state, inner in parts:
        operands += [*local[1:], *partials, state, *inner]
    for arrays in ahead:
        operands += arrays
    widths = [(len(parts) + extra) * GROUP * HEAD_DIM for extra in (len(ahead), 0, 0)]
    return pl.pallas_call(
        functools.partial(finish_kernel, scale, square, group, halves, len(ahead)),
        out_shape=out,
        in_specs=[IN_VMEM] * len(operands) + [ANYWHERE] * len(before),
        out_specs=[ANYWHERE] * 3,
        scratch_shapes=[pltpu.VMEM((rows, width), jnp.bfloat16) for width in widths]
        + [pltpu.SemaphoreType.DMA((len(parts) + len(ahead), GROUP // 2, 3))],
        input_output_aliases={len(operands) + i: i for i in range(len(before))},
        compiler_params=pltpu.CompilerParams(vmem_limit_bytes=(2 + 3 * len(parts) + len(ahead)) << 20),
        cost_estimate=LONG,
        name="finish",
    )(*operands, *before)


def on_device(queries, key_rows, value_rows, out_grad):
    count = lax.axis_size("seq")
    square = count == 8
    scale = (HEAD_DIM * queries.shape[0] * count) ** -0.5
    sources = [
        pltpu.with_memory_space_constraint(array, pltpu.HBM) for array in (queries, key_rows, value_rows, out_grad)
    ]

    def trade(value, distance):
        return lax.ppermute(value, "seq", [(i, i ^ distance) for i in range(count)])

    def run(kernel, out, operands, after):
        return call(kernel, out, operands, after, name=(kernel.func if hasattr(kernel, "func") else kernel).__name__)

    part_eo, local_em, start_o = states_first(square, sources)
    start_in = trade(start_o, 1)
    part_em, start = states_mine(square, local_em, (start_o,))
    after = (start,)
    if square:
        (sent,) = run(row_first_kernel, [PIECE], (start, start_in), ())
        row_first = trade(sent, 2)
        after = (sent,)

    part_lo, part_lm, rest_o, rest = states_second(square, sources, after)
    rest_in = trade(rest_o, 1)
    sums_e, sums_l = (start, start_in), (rest, rest_in)
    partials_lo = within(scale, part_lo[:4], (rest_o,))
    after = (partials_lo[0],)
    if square:
        (sent,) = run(row_second_kernel, [PIECE], sums_l, after)
        row_second = trade(sent, 2)
        partials_lm = within(scale, part_lm[:4], (sent,), range(GROUP // 4))
        sent, own_prefix, along = run(column_first_kernel, [PIECE] * 3, (*sums_l, row_first), (partials_lm[0],))
        column_first = trade(sent, 4)
        after = (sent,)
    else:
        partials_lm = within(scale, part_lm[:4], after, range(GROUP // 4))
        along = start

    part_eo, part_em, later_o, later = states_other(square, sources, part_eo, part_em, along, after)
    later_in = trade(later_o, 1)
    sums_b = (later, later_in)
    partials_lm = within(scale, part_lm[:4], (later_o,), range(GROUP // 4, GROUP // 2), partials_lm)
    partials_eo = within(scale, part_eo[:4], (partials_lm[0],))
    if square:
        (sent,) = run(column_second_kernel, [PIECE], (*sums_e, row_second), (partials_eo[0],))
        column_second = trade(sent, 4)
        (sent,) = run(row_third_kernel, [PIECE], (*sums_b, column_first), (sent,))
        row_third = trade(sent, 2)
        arrived = (row_second, column_first)
        own_e, other_e = run(first_states_kernel, STATES, (*sums_e, *sums_b, *arrived), (sent,))
    else:
        turns = range(1, count // 2)
        arrived = []
        sums = (*sums_e, *sums_b, *sums_l)
        for group in range(2):
            kernel = functools.partial(join_kernel, turns, group)
            sent = run(kernel, [PIECE] * len(turns), sums, (partials_eo[0],))
            arrived.append([trade(value, 2 * turn) for turn, value in zip(turns, sent, strict=True)])
        kernel = functools.partial(combine_kernel, turns, 0)
        own_e, other_e = run(kernel, STATES, (*sums, *arrived[0]), ())

    other_e = trade(other_e, 1)
    partials_em = within(scale, part_em[:4], (own_e,))
    parts = [(True, part_em[:4], partials_em, own_e, part_em[4:]), (False, part_eo[:4], partials_eo, other_e, part_eo[4:])]
    ahead = ()
    if square:
        ahead = (
            (part_lm[3], partials_lm[0], own_prefix, part_lm[4]),
            (part_lo[3], partials_lo[0], later_in, part_lo[4]),
        )
    done = finish(scale, square, 0, parts, (), ahead)

    after = (pltpu.with_memory_space_constraint(done[0], pltpu.HBM),)
    if square:
        arrived = (row_first, row_third, column_second)
        own_l, other_l = run(second_states_kernel, STATES, (*sums_l, *arrived), after)
    else:
        kernel = functools.partial(combine_kernel, turns, 1)
        own_l, other_l = run(kernel, STATES, (*sums, *arrived[1]), after)
    other_l = trade(other_l, 1)
    done = finish(scale, square, 1, [(True, part_lm[:4], partials_lm, own_l, part_lm[4:])], done)
    return tuple(finish(scale, square, 1, [(False, part_lo[:4], partials_lo, other_l, part_lo[4:])], done))


def solution(mesh):
    placed = P(("lists", "seq"), None)
    return jax.shard_map(
        on_device,
        mesh=mesh,
        in_specs=(placed,) * 4,
        out_specs=(placed,) * 3,
        check_vma=False,
    )
```

```python
import functools

import jax
import jax.numpy as jnp
from jax import lax
from jax.experimental import pallas as pl
from jax.experimental.pallas import tpu as pltpu
from jax.sharding import PartitionSpec as P

HEADS = 16
HEAD_DIM = 128
HALF = HEADS // 2
COLUMNS = HALF * HEAD_DIM
GROUP = HALF // 2
SUB = 256
PARTIAL = jnp.bfloat16

TN = (((0,), (0,)), ((), ()))
NT = (((1,), (1,)), ((), ()))
NN = (((1,), (0,)), ((), ()))

IN_VMEM = pl.BlockSpec(memory_space=pltpu.VMEM)
ANYWHERE = pl.BlockSpec(memory_space=pl.ANY)
SHORT = pl.CostEstimate(flops=1000, bytes_accessed=1000, transcendentals=0)
LONG = pl.CostEstimate(flops=2 * 10**10, bytes_accessed=1000, transcendentals=0)


def dot(left, right, dims):
    return lax.dot_general(left, right, dims, preferred_element_type=jnp.float32)


def state_of(heads):
    return pltpu.VMEM((2, heads, HEAD_DIM, HEAD_DIM), jnp.float32)


def head_columns(head):
    return pl.ds(head * HEAD_DIM, HEAD_DIM)


def my_core():
    return lax.rem(lax.axis_index("seq"), 2)


def my_pair():
    return lax.div(lax.axis_index("seq"), 2)


def first_column(square, mine, group):
    half = my_core() if mine else 1 - my_core()
    if square:
        pair = my_pair()
        group = jnp.where((pair == 1) | (pair == 2), 1 - group, group)
    return half * COLUMNS + group * (GROUP * HEAD_DIM)


def my_row(square):
    return lax.div(my_pair(), 2) if square else jnp.int32(0)


PIECE = pltpu.VMEM((GROUP, HEAD_DIM, HEAD_DIM), jnp.float32)
STATES = [state_of(GROUP)] * 2


def call(kernel, out, operands, after=(), scratch=(), cost=SHORT, limit=3, name=None):
    return pl.pallas_call(
        kernel,
        out_shape=out,
        in_specs=[IN_VMEM] * len(operands) + [ANYWHERE] * len(after),
        out_specs=[IN_VMEM] * len(out),
        scratch_shapes=list(scratch),
        compiler_params=pltpu.CompilerParams(vmem_limit_bytes=limit << 20),
        cost_estimate=cost,
        name=name,
    )(*operands, *after)


KINDS = ((1, 2), (0, 3))


def read(square, mine, group, kind, sources, local, sems):
    width = GROUP * HEAD_DIM
    at = pl.ds(pl.multiple_of(first_column(square, mine, group), width), width)
    return [pltpu.make_async_copy(sources[i].at[:, at], local[i], sems.at[i]) for i in KINDS[kind]]


def start_all(copies):
    for copy in copies:
        copy.start()


def sum_kind(kind, copies, local, sums, early, late):
    for copy in copies:
        copy.wait()
    q, k, v, o = local
    left, right = ((k, v), (q, o))[kind]
    subs = q.shape[0] // SUB
    order = list(range(subs)) if kind == 0 else list(range(subs - 1, -1, -1))
    for head in range(GROUP):
        at = head_columns(head)
        total = None
        for sub in order:
            span = pl.ds(sub * SUB, SUB)
            part = dot(left[span, at], right[span, at], TN)
            total = part if total is None else total + part
            if sub != order[-1]:
                if kind == 0:
                    early[head, sub] = total
                else:
                    late[head, sub - 1] = total
        sums[head] = total


def work_inside(scale, local, outs, pairs):
    (q, k, v, o), (dq, dk, dv) = local, outs
    rows = q.shape[0]
    part = SUB // 2
    at_row = lax.broadcasted_iota(jnp.int32, (SUB, SUB), 0)
    at_column = lax.broadcasted_iota(jnp.int32, (SUB, SUB), 1)
    lower = at_row >= at_column
    upper = at_row <= at_column
    nothing = jnp.zeros((part, HEAD_DIM), jnp.bfloat16)

    def weights_of(unit):
        pair, sub = unit
        span = pl.ds(sub * SUB, SUB)
        weights = []
        for head in (2 * pair, 2 * pair + 1):
            at = head_columns(head)
            grads = jnp.where(lower, scale * dot(o[span, at], v[span, at], NT), 0.0).astype(jnp.bfloat16)
            forward = jnp.where(upper, scale * dot(k[span, at], q[span, at], NT), 0.0).astype(jnp.bfloat16)
            weights.append((grads, grads.T, forward))
        return weights

    def side_by_side(weights, rows):
        left = jnp.concatenate([rows[0], nothing], axis=1)
        right = jnp.concatenate([nothing, rows[1]], axis=1)
        product = dot(jnp.concatenate(weights, axis=1), jnp.concatenate([left, right], axis=0), NN)
        return product[:, :HEAD_DIM], product[:, HEAD_DIM:]

    def lower_product(weights, rows):
        first = side_by_side([w[:part, :part] for w in weights], [r[:part] for r in rows])
        return [
            jnp.concatenate([top, dot(w[part:], r, NN)], axis=0) for top, w, r in zip(first, weights, rows, strict=True)
        ]

    def upper_product(weights, rows):
        last = side_by_side([w[part:, part:] for w in weights], [r[part:] for r in rows])
        return [
            jnp.concatenate([dot(w[:part], r, NN), below], axis=0) for below, w, r in zip(last, weights, rows, strict=True)
        ]

    units = [(pair, sub) for pair in pairs for sub in range(rows // SUB)]
    ahead = weights_of(units[0])
    for number, (pair, sub) in enumerate(units):
        grads, grads_t, forward = zip(*ahead, strict=True)
        if number + 1 < len(units):
            ahead = weights_of(units[number + 1])
        span = pl.ds(sub * SUB, SUB)
        places = [head_columns(2 * pair), head_columns(2 * pair + 1)]
        for product, weights, source, out in (
            (lower_product, grads, k, dq),
            (upper_product, grads_t, q, dk),
            (upper_product, forward, o, dv),
        ):
            for at, piece in zip(places, product(weights, [source[span, at] for at in places]), strict=True):
                out[span, at] = piece.astype(PARTIAL)


def part_shapes(rows):
    inner = pltpu.VMEM((GROUP, rows // SUB - 1, HEAD_DIM, HEAD_DIM), jnp.float32)
    return [pltpu.VMEM((rows, GROUP * HEAD_DIM), jnp.bfloat16)] * 4 + [inner] * 2


def states_first_kernel(square, *refs):
    sources, part, local, sums, sems = refs[:4], refs[4:10], refs[10:14], refs[14], refs[15]
    row = my_row(square)
    for kind in range(2):
        copies = read(square, False, 0, kind, sources, part[:4], sems.at[0])
        behind = read(square, True, 0, kind, sources, local, sems.at[1])

        @pl.when(row == kind)
        def _():
            start_all(copies)
            start_all(behind)
            sum_kind(kind, copies, part[:4], sums, *part[4:])
            for copy in behind:
                copy.wait()


def states_first(square, sources):
    part = part_shapes(sources[0].shape[0])
    out = part + part[:4] + [PIECE]
    result = pl.pallas_call(
        functools.partial(states_first_kernel, square),
        out_shape=out,
        in_specs=[ANYWHERE] * 4,
        out_specs=[IN_VMEM] * len(out),
        scratch_shapes=[pltpu.SemaphoreType.DMA((2, 4))],
        compiler_params=pltpu.CompilerParams(vmem_limit_bytes=2 << 20),
        cost_estimate=LONG,
        name="states_first",
    )(*sources)
    return result[:6], result[6:10], result[10]


def states_mine_kernel(square, *refs):
    local, inner, sums = refs[:4], refs[-3:-1], refs[-1]
    row = my_row(square)
    for kind in range(2):

        @pl.when(row == kind)
        def _():
            sum_kind(kind, (), local, sums, *inner)


def states_mine(square, local, after):
    inner = part_shapes(local[0].shape[0])[4:]
    out = [*inner, PIECE]
    kernel = functools.partial(states_mine_kernel, square)
    *inner, sums = call(kernel, out, local, after, cost=LONG, limit=2, name="states_mine")
    return [*local, *inner], sums


def states_second_kernel(square, *refs):
    sources, parts, sums, sems = refs[:4], (refs[-15:-9], refs[-9:-3]), refs[-3:-1], refs[-1]
    copies = {}
    for mine in range(2):
        for kind in range(2):
            copies[mine, kind] = read(square, bool(mine), 1, kind, sources, parts[mine][:4], sems.at[mine])
            start_all(copies[mine, kind])
    for mine in range(2):
        for kind in range(2):
            sum_kind(kind, copies[mine, kind], parts[mine][:4], sums[mine].at[kind], *parts[mine][4:])


def states_second(square, sources, after):
    out = part_shapes(sources[0].shape[0]) * 2 + [state_of(GROUP)] * 2
    result = pl.pallas_call(
        functools.partial(states_second_kernel, square),
        out_shape=out,
        in_specs=[ANYWHERE] * (4 + len(after)),
        out_specs=[IN_VMEM] * len(out),
        scratch_shapes=[pltpu.SemaphoreType.DMA((2, 4))],
        compiler_params=pltpu.CompilerParams(vmem_limit_bytes=2 << 20),
        cost_estimate=LONG,
        name="states_second",
    )(*sources, *after)
    return result[:6], result[6:12], *result[12:]


def states_other_kernel(square, *refs):
    sources, along, parts, sems = refs[:4], refs[16], (refs[-15:-9], refs[-9:-3]), refs[-1]
    sums = refs[-3].at[0], refs[-2]
    refs[-3][1] = along[...]
    row = my_row(square)
    copies = {}
    for mine in range(2):
        for kind in range(2):
            copies[mine, kind] = read(square, bool(mine), 0, kind, sources, parts[mine][:4], sems.at[mine])
    for kind in range(2):

        @pl.when(row != kind)
        def _():
            for mine in range(2):
                start_all(copies[mine, kind])
            for mine in range(2):
                sum_kind(kind, copies[mine, kind], parts[mine][:4], sums[mine], *parts[mine][4:])


def states_other(square, sources, other, mine, along, after):
    out = part_shapes(sources[0].shape[0]) * 2 + [state_of(GROUP), PIECE]
    result = pl.pallas_call(
        functools.partial(states_other_kernel, square),
        out_shape=out,
        in_specs=[ANYWHERE] * 4 + [IN_VMEM] * 13 + [ANYWHERE] * len(after),
        out_specs=[IN_VMEM] * len(out),
        scratch_shapes=[pltpu.SemaphoreType.DMA((2, 4))],
        input_output_aliases={4 + i: i for i in range(12)},
        compiler_params=pltpu.CompilerParams(vmem_limit_bytes=2 << 20),
        cost_estimate=LONG,
        name="states_other",
    )(*sources, *other, *mine, along, *after)
    return result[:6], result[6:12], *result[12:]


def within_kernel(scale, pairs, *refs):
    work_inside(scale, refs[:4], refs[-3:], pairs)


def within(scale, local, after, pairs=range(GROUP // 2), into=()):
    out = [pltpu.VMEM(local[0].shape, PARTIAL)] * 3
    return pl.pallas_call(
        functools.partial(within_kernel, scale, tuple(pairs)),
        out_shape=out,
        in_specs=[IN_VMEM] * (4 + len(into)) + [ANYWHERE] * len(after),
        out_specs=[IN_VMEM] * 3,
        input_output_aliases={4 + i: i for i in range(len(into))},
        compiler_params=pltpu.CompilerParams(vmem_limit_bytes=3 << 20),
        cost_estimate=LONG,
        name="within",
    )(*local, *into, *after)


def first_group(square, head, start, later):
    upper = my_row(square) == 0
    one, other = start[head], later[head]
    return jnp.where(upper, one, other), jnp.where(upper, other, one)


def second_group(head, rest):
    return rest[0, head], rest[1, head]


def settle(head, prefix, suffix, sums, sums_in, own, other):
    second = my_core() == 1
    own[0, head] = prefix + jnp.where(second, sums_in[0], 0.0)
    own[1, head] = suffix + jnp.where(second, 0.0, sums_in[1])
    other[0, head] = prefix + jnp.where(second, 0.0, sums[0])
    other[1, head] = suffix + jnp.where(second, sums[1], 0.0)


def comes_earlier(turn):
    pair = my_pair()
    return jnp.bitwise_xor(pair, turn) < pair


def sums_of_group(group, head, start, start_in, later, later_in, rest, rest_in):
    if group == 0:
        return first_group(False, head, start, later), first_group(False, head, start_in, later_in.at[0])
    return second_group(head, rest), second_group(head, rest_in)


def join_kernel(turns, group, *refs):
    for head in range(GROUP):
        sums, sums_in = sums_of_group(group, head, *refs[:6])
        for turn, out in zip(turns, refs[-len(turns) :], strict=True):
            out[head] = jnp.where(comes_earlier(turn), sums[1] + sums_in[1], sums[0] + sums_in[0])


def combine_kernel(turns, group, *refs):
    received = refs[6 : 6 + len(turns)]
    for head in range(GROUP):
        sums, sums_in = sums_of_group(group, head, *refs[:6])
        prefix = jnp.zeros((HEAD_DIM, HEAD_DIM), jnp.float32)
        suffix = jnp.zeros((HEAD_DIM, HEAD_DIM), jnp.float32)
        for turn, value in zip(turns, received, strict=True):
            earlier = comes_earlier(turn)
            prefix = prefix + jnp.where(earlier, value[head], 0.0)
            suffix = suffix + jnp.where(earlier, 0.0, value[head])
        settle(head, prefix, suffix, sums, sums_in, *refs[-2:])


def row_first_kernel(start, start_in, *refs):
    for head in range(GROUP):
        refs[-1][head] = start[head] + start_in[head]


def row_second_kernel(rest, rest_in, *refs):
    kind = lax.rem(my_pair(), 2)
    for head in range(GROUP):
        refs[-1][head] = rest[kind, head] + rest_in[kind, head]


def column_first_kernel(rest, rest_in, from_row, *refs):
    sent, own_prefix, other_prefix = refs[-3:]
    kind = my_row(True)
    second = my_core() == 1
    for head in range(GROUP):
        sent[head] = rest[kind, head] + rest_in[kind, head] + from_row[head]
        prefix = jnp.where(my_pair() == 1, from_row[head], 0.0)
        own_prefix[head] = prefix + jnp.where(second, rest_in[0, head], 0.0)
        other_prefix[head] = prefix + jnp.where(second, 0.0, rest[0, head])


def column_second_kernel(start, start_in, from_row, *refs):
    for head in range(GROUP):
        refs[-1][head] = start[head] + start_in[head] + from_row[head]


def row_third_kernel(later, later_in, from_column, *refs):
    pair = my_pair()
    outer = (pair == 0) | (pair == 3)
    for head in range(GROUP):
        refs[-1][head] = jnp.where(outer, from_column[head], later[head] + later_in[0, head])


def first_states_kernel(start, start_in, later, later_in, row_second, column_first, *refs):
    pair = my_pair()
    below, right = pair >= 2, lax.rem(pair, 2) == 1
    for head in range(GROUP):
        row, column = row_second[head], column_first[head]
        prefix = jnp.where(right, row, 0.0) + jnp.where(below, column, 0.0)
        suffix = jnp.where(right, 0.0, row) + jnp.where(below, 0.0, column)
        sums, sums_in = first_group(True, head, start, later), first_group(True, head, start_in, later_in.at[0])
        settle(head, prefix, suffix, sums, sums_in, *refs[-2:])


def second_states_kernel(rest, rest_in, row_first, row_third, column_second, *refs):
    pair = my_pair()
    below, outer = pair >= 2, (pair == 0) | (pair == 3)
    for head in range(GROUP):
        passed = row_third[head] + jnp.where(outer, column_second[head], 0.0)
        prefix = jnp.where(pair == 1, row_first[head], 0.0) + jnp.where(below, passed, 0.0)
        suffix = jnp.where(pair == 2, row_first[head], 0.0) + jnp.where(below, 0.0, passed)
        settle(head, prefix, suffix, second_group(head, rest), second_group(head, rest_in), *refs[-2:])


def add_state(scale, head, partial, rows, states, inner, dims, out, to):
    at = head_columns(head)
    subs = rows.shape[0] // SUB
    for sub in range(subs):
        span = pl.ds(sub * SUB, SUB)
        state = states[head]
        if dims[1] == 0:
            state = state + inner[head, sub - 1] if sub > 0 else state
        else:
            state = state + inner[head, sub] if sub < subs - 1 else state
        piece = partial[span, at] + scale * dot(rows[span, at], state.astype(jnp.bfloat16), dims[0])
        out[span, to] = piece.astype(jnp.bfloat16)


QUERY, KEY, VALUE = (NT, 0), (NT, 1), (NN, 1)


def finish_kernel(scale, square, group, halves, ahead, *refs):
    targets, staged, sems = refs[-7:-4], refs[-4:-1], refs[-1]
    row = my_row(square)

    def copies_of(i, number, which, first, heads):
        mine, at_group = halves[number % len(halves)], 1 if number >= len(halves) else group
        width = heads * HEAD_DIM
        column = first_column(square, mine, at_group) + first * HEAD_DIM
        return pltpu.make_async_copy(
            staged[i].at[:, pl.ds((number * GROUP + first) * HEAD_DIM, width)],
            targets[i].at[:, pl.ds(pl.multiple_of(column, HEAD_DIM), width)],
            sems.at[number, which, i],
        )

    def run(i, number, copies, partial, rows, states, inner, dims):
        for head in range(GROUP):
            to = head_columns(number * GROUP + head)
            add_state(scale, head, partial, rows, states, inner, dims, staged[i], to)
            if head % 2 == 1:
                copies[head // 2].start()

    def pieces(i, number):
        return [copies_of(i, number, which, 2 * which, 2) for which in range(GROUP // 2)]

    sometimes, always = [], []
    rest = refs[9 * len(halves) :]
    for n in range(ahead):
        number = len(halves) + n
        o, dq, prefix, early = rest[4 * n : 4 * n + 4]
        prefix = prefix if n == 0 else prefix.at[1]
        query = pieces(0, number)
        sometimes += query

        @pl.when(row == 0)
        def _():
            run(0, number, query, dq, o, prefix, early, QUERY)

    for number in range(len(halves)):
        k, v, o, dq, dk, dv, state, early, late = refs[9 * number : 9 * number + 9]
        query = pieces(0, number)
        if square and group == 1:
            sometimes += query

            @pl.when(row == 1)
            def _():
                run(0, number, query, dq, o, state.at[0], early, QUERY)
        else:
            always += query
            run(0, number, query, dq, o, state.at[0], early, QUERY)
        for i, arguments in ((1, (dk, v, state.at[1], late, KEY)), (2, (dv, k, state.at[1], late, VALUE))):
            copies = pieces(i, number)
            always += copies
            run(i, number, copies, *arguments)
    for copy in always:
        copy.wait()
    if sometimes:

        @pl.when(row == (0 if ahead else 1))
        def _():
            for copy in sometimes:
                copy.wait()


def finish(scale, square, group, parts, before, ahead=()):
    rows = parts[0][1][0].shape[0]
    out = [jax.ShapeDtypeStruct((rows, HEADS * HEAD_DIM), jnp.bfloat16)] * 3
    halves = tuple(part[0] for part in parts)
    operands = []
    for _, local, partials, state, inner in parts:
        operands += [*local[1:], *partials, state, *inner]
    for arrays in ahead:
        operands += arrays
    widths = [(len(parts) + extra) * GROUP * HEAD_DIM for extra in (len(ahead), 0, 0)]
    return pl.pallas_call(
        functools.partial(finish_kernel, scale, square, group, halves, len(ahead)),
        out_shape=out,
        in_specs=[IN_VMEM] * len(operands) + [ANYWHERE] * len(before),
        out_specs=[ANYWHERE] * 3,
        scratch_shapes=[pltpu.VMEM((rows, width), jnp.bfloat16) for width in widths]
        + [pltpu.SemaphoreType.DMA((len(parts) + len(ahead), GROUP // 2, 3))],
        input_output_aliases={len(operands) + i: i for i in range(len(before))},
        compiler_params=pltpu.CompilerParams(vmem_limit_bytes=(2 + 3 * len(parts) + len(ahead)) << 20),
        cost_estimate=LONG,
        name="finish",
    )(*operands, *before)


def on_device(queries, key_rows, value_rows, out_grad):
    count = lax.axis_size("seq")
    square = count == 8
    scale = (HEAD_DIM * queries.shape[0] * count) ** -0.5
    sources = [
        pltpu.with_memory_space_constraint(array, pltpu.HBM) for array in (queries, key_rows, value_rows, out_grad)
    ]

    def trade(value, distance):
        return lax.ppermute(value, "seq", [(i, i ^ distance) for i in range(count)])

    def run(kernel, out, operands, after):
        return call(kernel, out, operands, after, name=(kernel.func if hasattr(kernel, "func") else kernel).__name__)

    part_eo, local_em, start_o = states_first(square, sources)
    start_in = trade(start_o, 1)
    part_em, start = states_mine(square, local_em, (start_o,))
    after = (start,)
    if square:
        (sent,) = run(row_first_kernel, [PIECE], (start, start_in), ())
        row_first = trade(sent, 2)
        after = (sent,)

    part_lo, part_lm, rest_o, rest = states_second(square, sources, after)
    rest_in = trade(rest_o, 1)
    sums_e, sums_l = (start, start_in), (rest, rest_in)
    partials_lo = within(scale, part_lo[:4], (rest_o,))
    after = (partials_lo[0],)
    if square:
        (sent,) = run(row_second_kernel, [PIECE], sums_l, after)
        row_second = trade(sent, 2)
        partials_lm = within(scale, part_lm[:4], (sent,), range(GROUP // 4))
        sent, own_prefix, along = run(column_first_kernel, [PIECE] * 3, (*sums_l, row_first), (partials_lm[0],))
        column_first = trade(sent, 4)
        after = (sent,)
    else:
        partials_lm = within(scale, part_lm[:4], after, range(GROUP // 4))
        along = start

    part_eo, part_em, later_o, later = states_other(square, sources, part_eo, part_em, along, after)
    later_in = trade(later_o, 1)
    sums_b = (later, later_in)
    partials_lm = within(scale, part_lm[:4], (later_o,), range(GROUP // 4, GROUP // 2), partials_lm)
    partials_eo = within(scale, part_eo[:4], (partials_lm[0],))
    if square:
        (sent,) = run(column_second_kernel, [PIECE], (*sums_e, row_second), (partials_eo[0],))
        column_second = trade(sent, 4)
        (sent,) = run(row_third_kernel, [PIECE], (*sums_b, column_first), (sent,))
        row_third = trade(sent, 2)
        arrived = (row_second, column_first)
        own_e, other_e = run(first_states_kernel, STATES, (*sums_e, *sums_b, *arrived), (sent,))
    else:
        turns = range(1, count // 2)
        arrived = []
        sums = (*sums_e, *sums_b, *sums_l)
        for group in range(2):
            kernel = functools.partial(join_kernel, turns, group)
            sent = run(kernel, [PIECE] * len(turns), sums, (partials_eo[0],))
            arrived.append([trade(value, 2 * turn) for turn, value in zip(turns, sent, strict=True)])
        kernel = functools.partial(combine_kernel, turns, 0)
        own_e, other_e = run(kernel, STATES, (*sums, *arrived[0]), ())

    other_e = trade(other_e, 1)
    partials_em = within(scale, part_em[:4], (own_e,))
    parts = [(True, part_em[:4], partials_em, own_e, part_em[4:]), (False, part_eo[:4], partials_eo, other_e, part_eo[4:])]
    ahead = ()
    if square:
        ahead = (
            (part_lm[3], partials_lm[0], own_prefix, part_lm[4]),
            (part_lo[3], partials_lo[0], later_in, part_lo[4]),
        )
    done = finish(scale, square, 0, parts, (), ahead)

    after = (pltpu.with_memory_space_constraint(done[0], pltpu.HBM),)
    if square:
        arrived = (row_first, row_third, column_second)
        own_l, other_l = run(second_states_kernel, STATES, (*sums_l, *arrived), after)
    else:
        kernel = functools.partial(combine_kernel, turns, 1)
        own_l, other_l = run(kernel, STATES, (*sums, *arrived[1]), after)
    other_l = trade(other_l, 1)
    done = finish(scale, square, 1, [(True, part_lm[:4], partials_lm, own_l, part_lm[4:])], done)
    return tuple(finish(scale, square, 1, [(False, part_lo[:4], partials_lo, other_l, part_lo[4:])], done))


def solution(mesh):
    placed = P(("lists", "seq"), None)
    return jax.shard_map(
        on_device,
        mesh=mesh,
        in_specs=(placed,) * 4,
        out_specs=(placed,) * 3,
        check_vma=False,
    )
```
